32 devices in a mesh: pipe: 2 (over core), seq: 4 (over y, x), tensor: 4 (over z).
Axes of the slice: x: 2, y: 2, z: 4, core: 2. Of those that a mesh axis runs over, the one named last changes fastest.
Arguments:
- tokens: float32 [4, 4096, 800], P(None, 'seq'), may hold values from -6 to 6
- segments: int32 [4, 4096], P(None, 'seq'), may hold values from 0 to 15, as said below
- pad_mask: int32 [4, 4096], P(None, 'seq'), may hold values from 0 to 1, as said below
- cotangent: float32 [4, 4096, 800], P(None, 'seq'), may hold values from -6 to 6
- gain_first: float32 [2, 800], P('pipe'), may hold values from 0.1 to 1.9
- bias_first: float32 [2, 800], P('pipe'), may hold values from -3 to 3
- weight_inner: float32 [2, 800, 400], P('pipe', None, 'tensor'), may hold values from -0.21875 to 0.21875
- bias_inner: float32 [2, 400], P('pipe', 'tensor'), may hold values from -3 to 3
- gain_middle: float32 [2, 400], P('pipe', 'tensor'), may hold values from 0.1 to 1.9
- bias_middle: float32 [2, 400], P('pipe', 'tensor'), may hold values from -3 to 3
- weight_conv_encoder: float32 [5, 400, 400], P(None, None, 'tensor'), may hold values from -0.125 to 0.125
- weight_conv_decoder: float32 [3, 400, 400], P(None, None, 'tensor'), may hold values from -0.1875 to 0.1875
- bias_conv: float32 [2, 400], P('pipe', 'tensor'), may hold values from -3 to 3
- gain_last: float32 [2, 400], P('pipe', 'tensor'), may hold values from 0.1 to 1.9
- bias_last: float32 [2, 400], P('pipe', 'tensor'), may hold values from -3 to 3
- weight_outer: float32 [2, 400, 800], P('pipe', 'tensor'), may hold values from -0.3125 to 0.3125
- bias_outer: float32 [2, 800], P('pipe'), may hold values from -3 to 3
Outputs:
- section_output: float32 [2, 4, 4096, 800], P('pipe', None, 'seq')
- input_gradient: float32 [2, 4, 4096, 800], P('pipe', None, 'seq')
- grad_gain_first: float32 [2, 800], P('pipe')
- grad_bias_first: float32 [2, 800], P('pipe')
- grad_weight_inner: float32 [2, 800, 400], P('pipe', None, 'tensor')
- grad_bias_inner: float32 [2, 400], P('pipe', 'tensor')
- grad_gain_middle: float32 [2, 400], P('pipe', 'tensor')
- grad_bias_middle: float32 [2, 400], P('pipe', 'tensor')
- grad_conv_encoder: float32 [5, 400, 400], P(None, None, 'tensor')
- grad_conv_decoder: float32 [3, 400, 400], P(None, None, 'tensor')
- grad_bias_conv: float32 [2, 400], P('pipe', 'tensor')
- grad_gain_last: float32 [2, 400], P('pipe', 'tensor')
- grad_bias_last: float32 [2, 400], P('pipe', 'tensor')
- grad_weight_outer: float32 [2, 400, 800], P('pipe', 'tensor')
- grad_bias_outer: float32 [2, 800], P('pipe')
The draws below stay inside these ranges and needn't reach their ends.
Inputs may be any that keep to these rules, and one draw needn't show every extreme that they name: `segments`: along each row segment numbers start at 0 and never fall, rising by at most one; some row of every draw reaches 15. In every draw one row holds a segment that begins within its first 64 positions and lasts to the row's end. `pad_mask`: each row is 1 up to a padded tail of fewer than 64 positions, which are 0.
All inputs are finite; a program needn't handle non-finite values.
Results may differ from the reference program's by a relative error of at most 0.015.
Values may be sent and summed in bfloat16 or wider, within the bound.
No kernel may reach another device: no remote copies, remote signals or barrier semaphores. Data moves between devices by JAX's collectives and lax.ppermute only.
A program may use at most 320 MiB of HBM per device.

```python
import jax
import jax.numpy as jnp
from jax import lax

D = 800
H = 400
ENCODER_KERNEL = 5
DEC_TAPS = 3
ENCODER_SPACING = 16
LENGTH = 4096
ROWS = 4
N_PIPE = 2


def layout(key):
    pick_key, break_key, start_key, tail_key = jax.random.split(key, 4)
    edge = max(LENGTH // 64, 2)
    chosen = jax.random.randint(pick_key, (), 0, ROWS)
    other = (chosen + 1) % ROWS
    places = jnp.arange(LENGTH)[None, :]
    row_index = jnp.arange(ROWS)[:, None]
    breaks = jax.random.randint(break_key, (ROWS, LENGTH), 0, LENGTH) < 8
    regular = places % (LENGTH // 16) == 0
    breaks = jnp.where(row_index == other, regular, breaks)
    starts = jax.random.randint(start_key, (ROWS, 1), 1, edge)
    breaks = jnp.where(row_index == chosen, places == starts, breaks)
    breaks = breaks & (places > 0)
    numbers = jnp.minimum(jnp.cumsum(breaks.astype(jnp.int32), axis=1), 15).astype(jnp.int32)
    tails = jax.random.randint(tail_key, (ROWS, 1), 0, edge)
    mask = (places < LENGTH - tails).astype(jnp.int32)
    return (numbers, mask)


def draw_segments(key, part):
    numbers, mask = layout(key)
    return numbers


def draw_pad_mask(key, part):
    numbers, mask = layout(key)
    return mask


def block_scale(key, extent, shards, least, largest):
    def one(position, blocks):
        heights = jax.random.uniform(jax.random.fold_in(jax.random.fold_in(key, 6), position), (blocks,), jnp.float32, least / len(shards), largest / len(shards))
        return jnp.repeat(jnp.exp(heights), extent[position] // blocks).reshape((-1,) + (1,) * (len(extent) - position - 1))

    level = one(*shards[0])
    for cut in shards[1:]:
        level = level * one(*cut)
    return level


def noise(rng, extent, scale, reach, cuts=(), dtype=jnp.bfloat16):
    loudness = block_scale(rng, extent, cuts, -0.22, 0.18) if cuts else 1.0
    result = jax.random.normal(rng, extent, jnp.float32) * scale * loudness
    return jnp.minimum(jnp.maximum(result, -reach), reach).astype(dtype)


def setup_inputs(seed: int = 0) -> dict:
    arg_keys = jax.random.split(jax.random.key(seed), 18)
    return {
        "tokens": noise(arg_keys[0], (ROWS, LENGTH, D), 1.0, 6.0, ((1, 4),), jnp.float32),
        "segments": draw_segments(jax.random.fold_in(arg_keys[17], 71), 0),
        "pad_mask": draw_pad_mask(jax.random.fold_in(arg_keys[17], 71), 0),
        "cotangent": noise(arg_keys[3], (ROWS, LENGTH, D), 1.0, 6.0, ((1, 4),), jnp.float32),
        "gain_first": jnp.clip(1.0 + 0.18 * jax.random.normal(arg_keys[4], (N_PIPE, D), jnp.float32), 0.1, 1.9),
        "bias_first": noise(arg_keys[5], (N_PIPE, D), 0.5, 3.0, ((0, 2),), jnp.float32),
        "weight_inner": noise(arg_keys[6], (N_PIPE, D, H), D ** -0.5, 0.21875, ((0, 2), (2, 4)), jnp.float32),
        "bias_inner": noise(arg_keys[7], (N_PIPE, H), 0.5, 3.0, ((0, 2), (1, 4)), jnp.float32),
        "gain_middle": jnp.clip(1.0 + 0.18 * jax.random.normal(arg_keys[8], (N_PIPE, H), jnp.float32), 0.1, 1.9),
        "bias_middle": noise(arg_keys[9], (N_PIPE, H), 0.5, 3.0, ((0, 2), (1, 4)), jnp.float32),
        "weight_conv_encoder": noise(arg_keys[10], (ENCODER_KERNEL, H, H), (ENCODER_KERNEL * H) ** -0.5, 0.125, ((2, 4),), jnp.float32),
        "weight_conv_decoder": noise(arg_keys[11], (DEC_TAPS, H, H), (DEC_TAPS * H) ** -0.5, 0.1875, ((2, 4),), jnp.float32),
        "bias_conv": noise(arg_keys[12], (N_PIPE, H), 0.5, 3.0, ((0, 2), (1, 4)), jnp.float32),
        "gain_last": jnp.clip(1.0 + 0.18 * jax.random.normal(arg_keys[13], (N_PIPE, H), jnp.float32), 0.1, 1.9),
        "bias_last": noise(arg_keys[14], (N_PIPE, H), 0.5, 3.0, ((0, 2), (1, 4)), jnp.float32),
        "weight_outer": noise(arg_keys[15], (N_PIPE, H, D), H ** -0.5, 0.3125, ((0, 2), (1, 4)), jnp.float32),
        "bias_outer": noise(arg_keys[16], (N_PIPE, D), 0.5, 3.0, ((0, 2),), jnp.float32),
    }


@jax.custom_vjp
def low(v):
    return lax.optimization_barrier(v.astype(jnp.bfloat16)).astype(jnp.float32)

@jax.custom_vjp
def low_back(v):
    return v

def low_keep(v):
    return (low(v), None)

def low_pass(kept, grad):
    return (grad,)

def back_keep(v):
    return (v, None)

def back_low(kept, grad):
    return (low(grad),)
low.defvjp(low_keep, low_pass)
low_back.defvjp(back_keep, back_low)
EPSILON = 1e-05

def matmul(left, right):
    return jnp.dot(left, right, precision=lax.Precision.HIGHEST)

def normalize(values, gain, bias):
    center = lax.optimization_barrier(jnp.mean(values, axis=-1, keepdims=True))
    spread = lax.optimization_barrier(jnp.mean(values * values, axis=-1, keepdims=True)) - center * center
    return (values - center) * lax.rsqrt(spread + EPSILON) * gain + bias

def smooth(values):
    return jax.nn.gelu(values, approximate=True)

def block(inputs, params, codes, keep, tap_shifts):
    first_scale, first_shift, inner_matrix, inner_shift, middle_scale, middle_shift, conv_matrix, conv_shift, last_scale, last_shift, outer_matrix, outer_shift = params
    receptive_span = 2 * ENCODER_SPACING
    first = low(smooth(normalize(inputs, first_scale, first_shift)))
    hidden = low_back(matmul(first, low(inner_matrix))) + inner_shift
    second = low(smooth(normalize(hidden, middle_scale, middle_shift)))
    padded = jnp.pad(second, ((receptive_span, receptive_span), (0, 0)))
    padded_codes = jnp.pad(codes, (receptive_span, receptive_span))
    conv_low = low(conv_matrix)
    total = jnp.zeros((LENGTH, conv_matrix.shape[2]), jnp.float32)
    for index, offset in enumerate(tap_shifts):
        source = padded[receptive_span + offset:receptive_span + offset + LENGTH]
        valid = (padded_codes[receptive_span + offset:receptive_span + offset + LENGTH] == codes).astype(jnp.float32)
        total = total + matmul(source * valid[:, None], conv_low[index])
    mixed = low_back(total) + conv_shift
    third = low(smooth(normalize(mixed, last_scale, last_shift)))
    branch = (low_back(matmul(third, low(outer_matrix))) + outer_shift) * keep[:, None]
    return inputs + branch

def reference(tokens, segments, pad_mask, cotangent, gain_first, bias_first, weight_inner, bias_inner, gain_middle, bias_middle, weight_conv_encoder, weight_conv_decoder, bias_conv, gain_last, bias_last, weight_outer, bias_outer):
    before = (gain_first, bias_first, weight_inner, bias_inner, gain_middle, bias_middle)
    after = (bias_conv, gain_last, bias_last, weight_outer, bias_outer)
    params_encoder = tuple((p[0] for p in before)) + (weight_conv_encoder,) + tuple((p[0] for p in after))
    params_decoder = tuple((p[1] for p in before)) + (weight_conv_decoder,) + tuple((p[1] for p in after))
    encoder_tap_shifts = [ENCODER_SPACING * (tap_number - 2) for tap_number in range(ENCODER_KERNEL)]
    decoder_offsets = [tap_number - (DEC_TAPS - 1) for tap_number in range(DEC_TAPS)]
    stacked_params = before + after

    def row_step(totals, row):
        section_totals, conv_encoder_total, conv_decoder_total = totals
        inputs, seg_row, mask_row, grad_row = row
        codes = jnp.where(mask_row == 1, seg_row + 1, 0).astype(jnp.int32)
        keep = mask_row.astype(jnp.float32)
        middle, back_encoder = jax.vjp(lambda v, p: block(v, p, codes, keep, encoder_tap_shifts), inputs, params_encoder)
        output, back_decoder = jax.vjp(lambda v, p: block(v, p, codes, keep, decoder_offsets), middle, params_decoder)
        grad_middle, grads_decoder = back_decoder(grad_row)
        grad_inputs, grads_encoder = back_encoder(grad_middle)
        encoder_rest = grads_encoder[:6] + grads_encoder[7:]
        decoder_rest = grads_decoder[:6] + grads_decoder[7:]
        section_totals = tuple((t + jnp.stack([a, b]) for t, a, b in zip(section_totals, encoder_rest, decoder_rest)))
        totals = (section_totals, conv_encoder_total + grads_encoder[6], conv_decoder_total + grads_decoder[6])
        return (totals, (middle, output, grad_inputs, grad_middle))
    start = (tuple((jnp.zeros(p.shape, jnp.float32) for p in stacked_params)), jnp.zeros(weight_conv_encoder.shape, jnp.float32), jnp.zeros(weight_conv_decoder.shape, jnp.float32))
    totals, stacked = lax.scan(row_step, start, (tokens, segments, pad_mask, cotangent))
    section_totals, conv_encoder_total, conv_decoder_total = totals
    middles, outputs, grad_inputs, grad_middles = stacked
    section_output = jnp.stack([middles, outputs])
    input_gradient = jnp.stack([grad_inputs, grad_middles])
    return (section_output, input_gradient, section_totals[0], section_totals[1], section_totals[2], section_totals[3], section_totals[4], section_totals[5], conv_encoder_total, conv_decoder_total, section_totals[6], section_totals[7], section_totals[8], section_totals[9], section_totals[10])
```

```python
import functools
import math

import jax
import jax.numpy as jnp
from jax import lax
from jax.experimental import pallas as pl
from jax.experimental.pallas import tpu as pltpu
from jax.sharding import PartitionSpec as P

SPACING = 16
EPSILON = 1e-05
BF = jnp.bfloat16
F32 = jnp.float32
LANES = 512
ROOT = math.sqrt(2.0 / math.pi)
CUBIC = 0.044715
E_OFFSETS = tuple(SPACING * (k - 2) for k in range(5))
D_OFFSETS = (-2, -1, 0)
COLUMN = {-32: 0, -16: 1, 16: 2, 32: 3, -2: 4, -1: 5, 2: 6, 1: 7}
KEEP, OWN = 8, 9
TOK, MID, COT = 96, 64, 32


def dot(a, b):
    return lax.dot_general(a, b, (((1,), (0,)), ((), ())), preferred_element_type=F32)


def dot_nt(a, b):
    return lax.dot_general(a, b, (((1,), (1,)), ((), ())), preferred_element_type=F32)


def dot_tn(a, b):
    return lax.dot_general(a, b, (((0,), (0,)), ((), ())), preferred_element_type=F32)


def normalized(values, width):
    center = jnp.sum(values, axis=-1, keepdims=True) * (1.0 / width)
    square = jnp.sum(values * values, axis=-1, keepdims=True) * (1.0 / width)
    inverse = lax.rsqrt(square - center * center + EPSILON)
    return (values - center) * inverse, inverse


def gate(half):
    square = half * half
    return jnp.tanh(half * (2 * ROOT + (8 * CUBIC * ROOT) * square)), square


def slope(half, tanh, square):
    return (1.0 + tanh) * (0.5 + half * (1.0 - tanh) * (ROOT + (12 * CUBIC * ROOT) * square))


def activated(scaled, gain, bias):
    half = scaled * (0.5 * gain) + 0.5 * bias
    tanh, square = gate(half)
    return half + half * tanh, slope(half, tanh, square)


def back(weighted, scaled, inverse, width):
    first = jnp.sum(weighted, axis=-1, keepdims=True) * (1.0 / width)
    second = jnp.sum(weighted * scaled, axis=-1, keepdims=True) * (1.0 / width)
    return inverse * (weighted - first - scaled * second)


def rows8(values):
    count, width = values.shape
    return jnp.sum(values.reshape(count // 8, 8, width), axis=0)


def first_step():
    return (pl.program_id(0) == 0) & (pl.program_id(1) == 0)


def masked(values, mask_ref, offset):
    column = mask_ref[0, :, COLUMN[offset] : COLUMN[offset] + 1].astype(BF)
    return values * column


def middle(hidden, h_ref, row, inner, sec_ref, xh_ref, dg_ref, inv_ref):
    scaled, inverse = normalized(hidden, inner)
    value, grad = activated(scaled, h_ref[row : row + 1, :], h_ref[row + 1 : row + 2, :])
    if sec_ref is not None:
        sec_ref[0] = value.astype(BF)
    xh_ref[0] = scaled.astype(BF)
    dg_ref[0] = grad.astype(BF)
    inv_ref[0] = jnp.broadcast_to(inverse, inv_ref.shape[1:])
    return value.astype(BF)


def encoder_in(inner, meta, tok_ref, wi_ref, d_ref, h_ref, sec_ref, xh_ref, dg_ref, inv_ref):
    values = tok_ref[0]
    scaled, _ = normalized(values, values.shape[-1])
    half = scaled * (0.5 * d_ref[0:1, :]) + 0.5 * d_ref[1:2, :]
    tanh, _ = gate(half)
    first = (half + half * tanh).astype(BF)
    hidden = dot(first, wi_ref[...]) + h_ref[0:1, :]
    middle(hidden, h_ref, 1, inner, sec_ref, xh_ref, dg_ref, inv_ref)


def encoder_out(
    inner, chunk, meta, sec_ref, tok_ref, mask_ref, wc_ref, wo_ref, wi_ref, de_ref, he_ref, dd_ref, hd_ref,
    out_ref, xh3_ref, dg3_ref, inv3_ref, third_ref, sec2_ref, xh2_ref, dg2_ref, inv2_ref, keep_ref,
):
    start = pl.program_id(1) * chunk + (TOK - MID)
    total = None
    for k, offset in enumerate(E_OFFSETS):
        piece = sec_ref[0, pl.ds(pl.multiple_of(start + offset, 16), chunk), :]
        if offset:
            piece = masked(piece, mask_ref, offset)
        term = dot(piece, wc_ref[k])
        total = term if total is None else total + term
    mixed = total + he_ref[3:4, :]
    third = middle(mixed, he_ref, 4, inner, None, xh3_ref, dg3_ref, inv3_ref)
    keep_ref[...] = third
    third_ref[0] = keep_ref[:, pl.ds(pl.multiple_of(meta[1] * 128, 128), 128)]
    keep = mask_ref[0, :, KEEP : KEEP + 1]
    output = tok_ref[0] + keep * (dot(third, wo_ref[...]) + de_ref[2:3, :])
    out_ref[0] = output
    scaled, _ = normalized(output, output.shape[-1])
    half = scaled * (0.5 * dd_ref[0:1, :]) + 0.5 * dd_ref[1:2, :]
    tanh, _ = gate(half)
    first = (half + half * tanh).astype(BF)
    hidden = dot(first, wi_ref[...]) + hd_ref[0:1, :]
    middle(hidden, hd_ref, 1, inner, sec2_ref, xh2_ref, dg2_ref, inv2_ref)


def add_to(ref, value):
    ref[...] += value


def decoder_out(
    inner, chunk, length, meta, sec_ref, in_ref, cot_ref, mask_ref, wc_ref, wo_ref, dd_ref, hd_ref, final_ref,
    mine_ref, other_ref, mixed_ref, go_ref, gc_ref, gd_ref, gh_ref,
    third_ref, low_ref, mine_buf, other_buf, sems,
):
    del final_ref
    row, step = pl.program_id(0), pl.program_id(1)
    steps = pl.num_programs(1)

    @pl.when(first_step())
    def _():
        for ref in (go_ref, gc_ref, gd_ref, gh_ref):
            ref[...] = jnp.zeros_like(ref)

    start = pl.multiple_of(step * chunk + (MID - COT - 16), 16)
    window = sec_ref[0, pl.ds(start, chunk + 16), :].astype(F32)
    pieces = []
    total = None
    for k, offset in enumerate(D_OFFSETS):
        piece = window[16 + offset : 16 + offset + chunk].astype(BF)
        if offset:
            piece = masked(piece, mask_ref, offset)
        pieces.append(piece)
        term = dot(piece, wc_ref[k])
        total = term if total is None else total + term
    mixed = total + hd_ref[3:4, :]
    scaled, inverse = normalized(mixed, inner)
    value, grad = activated(scaled, hd_ref[4:5, :], hd_ref[5:6, :])
    third = value.astype(BF)
    keep = mask_ref[0, :, KEEP : KEEP + 1]
    own = mask_ref[0, :, OWN : OWN + 1]
    inputs = in_ref[0]
    output = inputs + keep * (dot(third, wo_ref[...]) + dd_ref[2:3, :])
    encoder_side = meta[0] == 0
    at = pl.ds(pl.multiple_of(step * chunk, 16), chunk)
    mine_buf[row, at, :] = jnp.where(encoder_side, inputs, output)
    other_buf[row, at, :] = jnp.where(encoder_side, output, inputs).astype(BF)

    branch = keep * cot_ref[0]
    branch_low = branch.astype(BF)
    gd_ref[0:8, :] += rows8(branch * own)
    grad_third = dot_nt(branch_low, wo_ref[...])
    grad_normed = grad * grad_third
    kept = grad_normed * own
    gh_ref[0:8, :] += rows8(kept * scaled)
    gh_ref[8:16, :] += rows8(kept)
    grad_mixed = back(grad_normed * hd_ref[4:5, :], scaled, inverse, inner)
    gh_ref[16:24, :] += rows8(grad_mixed * own)
    mixed_low = grad_mixed.astype(BF)
    mixed_ref[0] = mixed_low
    third_ref[...] = third
    low_ref[...] = mixed_low
    lanes = pl.ds(pl.multiple_of(meta[1] * 128, 128), 128)
    own_low = own.astype(BF)
    go_ref[...] += dot_tn(third_ref[:, lanes] * own_low, branch_low)
    mixed_own = low_ref[:, lanes] * own_low
    for k in range(3):
        gc_ref[k] += dot_tn(mixed_own, pieces[k])

    @pl.when(step == steps - 1)
    def _():
        target = meta[0] * pl.num_programs(0) + row
        pltpu.make_async_copy(mine_buf.at[row, COT : COT + length], mine_ref.at[target], sems.at[0, row]).start()
        pltpu.make_async_copy(other_buf.at[row, COT : COT + length], other_ref.at[row], sems.at[1, row]).start()

    @pl.when((step == steps - 1) & (row == pl.num_programs(0) - 1))
    def _():
        for r in range(mine_buf.shape[0]):
            target = meta[0] * pl.num_programs(0) + r
            pltpu.make_async_copy(mine_buf.at[r, COT : COT + length], mine_ref.at[target], sems.at[0, r]).wait()
            pltpu.make_async_copy(other_buf.at[r, COT : COT + length], other_ref.at[r], sems.at[1, r]).wait()


def inner_back(
    inner, grad_second, xh_ref, dg_ref, inv_ref, h_ref, wi_ref, inputs, d_ref, own, lanes, low_ref,
    gi_ref, gd_ref, gh_ref, base,
):
    scaled = xh_ref[0].astype(F32)
    inverse = inv_ref[0][:, 0:1]
    grad_normed = dg_ref[0].astype(F32) * grad_second
    kept = grad_normed if own is None else grad_normed * own
    gh_ref[base : base + 8, :] += rows8(kept * scaled)
    gh_ref[base + 8 : base + 16, :] += rows8(kept)
    grad_hidden = back(grad_normed * h_ref[1:2, :], scaled, inverse, inner)
    gh_ref[base + 16 : base + 24, :] += rows8(grad_hidden if own is None else grad_hidden * own)
    hidden_low = grad_hidden.astype(BF)
    low_ref[...] = hidden_low
    width = inputs.shape[-1]
    scaled1, inverse1 = normalized(inputs, width)
    value, grad = activated(scaled1, d_ref[0:1, :], d_ref[1:2, :])
    mine = low_ref[:, lanes]
    if own is not None:
        mine = mine * own.astype(BF)
    gi_ref[...] += dot_tn(mine, value.astype(BF))
    grad_normed1 = grad * dot_nt(hidden_low, wi_ref[...])
    kept = grad_normed1 if own is None else grad_normed1 * own
    gd_ref[0:8, :] += rows8(kept * scaled1)
    gd_ref[8:16, :] += rows8(kept)
    return back(grad_normed1 * d_ref[0:1, :], scaled1, inverse1, width)


def decoder_back(
    inner, chunk, meta, mixed_ref, xh2_ref, dg2_ref, inv2_ref, in_ref, cot_ref, mask_ref, wc_ref, wi_ref, dd_ref, hd_ref,
    xh3_ref, dg3_ref, inv3_ref, third_ref, wo_ref, he_ref,
    grad_ref, low3_ref, gi_ref, gd_ref, gh_ref, go_ref, gde_ref, ghe_ref,
    low_ref,
):
    @pl.when(first_step())
    def _():
        for ref in (gi_ref, gd_ref, gh_ref, go_ref, gde_ref, ghe_ref):
            ref[...] = jnp.zeros_like(ref)

    lanes = pl.ds(pl.multiple_of(meta[1] * 128, 128), 128)
    own = mask_ref[0, :, OWN : OWN + 1]
    start = pl.multiple_of(pl.program_id(1) * chunk, 16)
    window = mixed_ref[0, pl.ds(start, chunk + 16), :].astype(F32)
    total = None
    for k, offset in enumerate(D_OFFSETS):
        piece = window[-offset : chunk - offset].astype(BF)
        if offset:
            piece = masked(piece, mask_ref, -offset)
        term = dot_nt(piece, wc_ref[k])
        total = term if total is None else total + term
    grad_inputs = cot_ref[0] + inner_back(
        inner, total, xh2_ref, dg2_ref, inv2_ref, hd_ref, wi_ref, in_ref[0], dd_ref, own, lanes, low_ref,
        gi_ref, gd_ref, gh_ref, 0,
    )
    grad_ref[0] = grad_inputs
    branch = mask_ref[0, :, KEEP : KEEP + 1] * grad_inputs
    branch_low = branch.astype(BF)
    gde_ref[...] += rows8(branch * own)
    go_ref[...] += dot_tn(third_ref[0] * own.astype(BF), branch_low)
    scaled = xh3_ref[0].astype(F32)
    grad_normed = dg3_ref[0].astype(F32) * dot_nt(branch_low, wo_ref[...])
    kept = grad_normed * own
    ghe_ref[0:8, :] += rows8(kept * scaled)
    ghe_ref[8:16, :] += rows8(kept)
    grad_mixed = back(grad_normed * he_ref[4:5, :], scaled, inv3_ref[0][:, 0:1], inner)
    ghe_ref[16:24, :] += rows8(grad_mixed * own)
    low3_ref[0] = grad_mixed.astype(BF)


def encoder_back(
    inner, chunk, meta, mixed_ref, sec_ref, xh2_ref, dg2_ref, inv2_ref, in_ref, grad_ref, mask_ref, wc_ref, wi_ref, de_ref,
    he_ref, final_ref,
    mine_ref, other_ref, gi_ref, gc_ref, gd_ref, gh_ref,
    low_ref,
):
    del final_ref

    @pl.when(first_step())
    def _():
        for ref in (gi_ref, gc_ref, gd_ref, gh_ref):
            ref[...] = jnp.zeros_like(ref)

    lanes = pl.ds(pl.multiple_of(meta[1] * 128, 128), 128)
    step = pl.program_id(1)
    total = None
    for k, offset in enumerate(E_OFFSETS):
        piece = mixed_ref[0, pl.ds(pl.multiple_of(step * chunk + COT - offset, 16), chunk), :]
        if offset:
            piece = masked(piece, mask_ref, -offset)
        term = dot_nt(piece, wc_ref[k])
        total = term if total is None else total + term
    mixed_own = mixed_ref[0, pl.ds(pl.multiple_of(step * chunk + COT, 16), chunk), lanes]
    for k, offset in enumerate(E_OFFSETS):
        piece = sec_ref[0, pl.ds(pl.multiple_of(step * chunk + TOK + offset, 16), chunk), :]
        if offset:
            piece = masked(piece, mask_ref, offset)
        gc_ref[k] += dot_tn(mixed_own, piece)
    later = grad_ref[0]
    result = later + inner_back(
        inner, total, xh2_ref, dg2_ref, inv2_ref, he_ref, wi_ref, in_ref[0], de_ref, None, lanes, low_ref,
        gi_ref, gd_ref, gh_ref, 0,
    )
    encoder_side = meta[0] == 0
    mine_ref[0] = jnp.where(encoder_side, result, later)
    other_ref[0] = jnp.where(encoder_side, later, result).astype(BF)


def fill_rows(meta, recv_ref, final_ref, out_ref):
    del meta, final_ref
    out_ref[0] = recv_ref[0].astype(F32)


def call(body, meta, grid, ins, outs, scratch=(), aliases=None, name=None, flops=0, nbytes=0):
    args = [a for a, _ in ins]
    return pl.pallas_call(
        body,
        grid_spec=pltpu.PrefetchScalarGridSpec(
            num_scalar_prefetch=1,
            grid=grid,
            in_specs=[s for _, s in ins],
            out_specs=[s for _, s in outs],
            scratch_shapes=list(scratch),
        ),
        out_shape=[s for s, _ in outs],
        input_output_aliases=aliases or {},
        compiler_params=pltpu.CompilerParams(
            dimension_semantics=("arbitrary",) * len(grid), vmem_limit_bytes=58 * 1024 * 1024
        ),
        cost_estimate=pl.CostEstimate(flops=flops, bytes_accessed=nbytes, transcendentals=0),
        name=name,
    )(meta, *args)


def blocked(array, rows):
    return (array, pl.BlockSpec((1, rows, array.shape[2]), lambda r, i, m: (r, i, 0)))


def element(array, rows, base):
    return (
        array,
        pl.BlockSpec(
            (pl.Element(1), pl.Element(rows), pl.Element(array.shape[2])), lambda r, i, m: (r, pl.multiple_of(i * rows + base, 16), 0)
        ),
    )


def whole_row(array):
    return (array, pl.BlockSpec((1,) + array.shape[1:], lambda r, i, m: (r, 0, 0)))


def fixed(array):
    zeros = (0,) * array.ndim
    return (array, pl.BlockSpec(array.shape, lambda r, i, m: zeros))


def out_blocked(count, total, rows, width, dtype):
    return (
        jax.ShapeDtypeStruct((count, total, width), dtype),
        pl.BlockSpec((1, rows, width), lambda r, i, m: (r, i, 0)),
    )


def out_fixed(shape):
    zeros = (0,) * len(shape)
    return (jax.ShapeDtypeStruct(shape, F32), pl.BlockSpec(shape, lambda r, i, m: zeros))


def flip(x, axis, by):
    count = lax.axis_size(axis)
    return lax.ppermute(x, axis, [(i, i ^ by) for i in range(count)])


def gather(x, axis):
    me = lax.axis_index(axis)
    count = lax.axis_size(axis)
    result = jnp.zeros((count,) + x.shape, x.dtype)
    result = lax.dynamic_update_index_in_dim(result, x, me, 0)
    for by in range(1, count):
        result = lax.dynamic_update_index_in_dim(result, flip(x, axis, by), me ^ by, 0)
    return result


def sum_over(x, axis):
    count = lax.axis_size(axis)
    me = lax.axis_index(axis)
    parts = x.reshape((count, x.shape[0] // count) + x.shape[1:])
    low = parts.astype(BF)
    total = lax.dynamic_index_in_dim(parts, me, 0, keepdims=False)
    for by in range(1, count):
        total = total + flip(lax.dynamic_index_in_dim(low, me ^ by, 0, keepdims=False), axis, by).astype(F32)
    return gather(total.astype(BF), axis).astype(F32).reshape(x.shape)


def pad_to(x, axis, size):
    widths = [(0, 0)] * x.ndim
    widths[axis] = (0, size - x.shape[axis])
    return jnp.pad(x, widths)


def on_device(
    tokens, segments, pad_mask, cotangent, gain_first, bias_first, weight_inner, bias_inner, gain_middle, bias_middle,
    weight_conv_encoder, weight_conv_decoder, bias_conv, gain_last, bias_last, weight_outer, bias_outer,
):
    pipe, seq, tensor = (lax.axis_index(a) for a in ("pipe", "seq", "tensor"))
    n_pipe, n_seq, n_tensor = (lax.axis_size(a) for a in ("pipe", "seq", "tensor"))
    rows_all, length, width = tokens.shape
    rows = rows_all // n_pipe
    local = weight_conv_encoder.shape[2]
    inner = weight_conv_encoder.shape[1]
    lanes = LANES // n_tensor
    encoder_side = pipe == 0
    meta = jnp.stack([pipe, tensor * lanes // 128]).astype(jnp.int32)

    def mine_rows(array):
        return lax.dynamic_slice_in_dim(array, pipe * rows, rows, 0)

    def quarter(array, axis):
        size = array.shape[axis] // n_seq
        return lax.dynamic_slice_in_dim(array, seq * size, size, axis)

    small = jnp.stack([bias_inner[0], gain_middle[0], bias_middle[0], bias_conv[0], gain_last[0], bias_last[0]])
    small = gather(pad_to(pad_to(small, 1, lanes), 0, 8), "tensor")
    small = jnp.transpose(small, (1, 0, 2)).reshape(8, LANES)
    large = pad_to(jnp.stack([gain_first[0], bias_first[0], bias_outer[0]]), 0, 8)
    small2, large2 = flip(small, "pipe", 1), flip(large, "pipe", 1)
    he, hd = jnp.where(encoder_side, small, small2), jnp.where(encoder_side, small2, small)
    de, dd = jnp.where(encoder_side, large, large2), jnp.where(encoder_side, large2, large)

    def both(full):
        other = flip(full, "pipe", 1)
        return jnp.where(encoder_side, full, other), jnp.where(encoder_side, other, full)

    in_piece = pad_to(quarter(weight_inner[0].astype(BF), 0), 1, lanes)
    in_all = gather(gather(in_piece, "tensor"), "seq")
    in_full = jnp.transpose(in_all, (0, 2, 1, 3)).reshape(width, LANES)
    inner_e, inner_d = both(in_full)

    conv_mine = jnp.where(
        encoder_side,
        weight_conv_encoder[:4],
        jnp.concatenate([weight_conv_encoder[4:], weight_conv_decoder], axis=0),
    ).astype(BF)
    conv_mine = pad_to(conv_mine.reshape(4, n_tensor, local, local), 3, lanes)
    conv_mine = pad_to(conv_mine, 2, lanes).reshape(4, LANES, lanes)
    conv_all = gather(gather(quarter(conv_mine, 1), "tensor"), "seq")
    conv_full = jnp.transpose(conv_all, (2, 0, 3, 1, 4)).reshape(4, LANES, LANES)
    conv_a, conv_b = both(conv_full)
    conv_e = jnp.concatenate([conv_a, conv_b[:1]], axis=0)
    conv_d = conv_b[1:]

    out_piece = quarter(pad_to(weight_outer[0].astype(BF), 0, lanes), 0)
    out_all = gather(gather(out_piece, "tensor"), "seq")
    out_full = jnp.transpose(out_all, (1, 0, 2, 3)).reshape(LANES, width)
    outer_e, outer_d = both(out_full)

    def neighbours(array, reach):
        right = [(i, i + 1) for i in range(n_seq - 1)]
        left = [(i + 1, i) for i in range(n_seq - 1)]
        before = lax.ppermute(array[:, length - reach :], "seq", right)
        after = lax.ppermute(array[:, :reach], "seq", left)
        return before, after

    tokens_mine, cotangent_mine = mine_rows(tokens), mine_rows(cotangent)
    before, after = neighbours(tokens_mine.astype(BF), 80)
    ends = jnp.zeros((rows, TOK - 80, width), F32)
    tok_ext = jnp.concatenate([ends, before.astype(F32), tokens_mine, after.astype(F32), ends], axis=1)
    before, after = neighbours(cotangent_mine.astype(BF), 48)
    cot_ext = jnp.concatenate(
        [before[:, 48 - COT :].astype(F32), cotangent_mine, after.astype(F32)], axis=1
    )
    codes = mine_rows(jnp.where(pad_mask == 1, segments + 1, 0)) + 1
    before, after = neighbours(codes, 128)
    codes = jnp.concatenate([before, codes, after], axis=1) - 1
    total = length + 2 * TOK
    here = codes[:, 128 - TOK : 128 - TOK + total]
    columns = [None] * 16
    for offset, index in COLUMN.items():
        there = codes[:, 128 - TOK + offset : 128 - TOK + offset + total]
        columns[index] = (there == here).astype(F32)
    columns[KEEP] = (here > 0).astype(F32)
    place = jnp.arange(total)
    columns[OWN] = jnp.broadcast_to(((place >= TOK) & (place < TOK + length)).astype(F32), here.shape)
    for index in range(10, 16):
        columns[index] = jnp.zeros_like(columns[0])
    masks = jnp.stack(columns, axis=-1)

    n1, n2, n3, n4, n5 = 4, 4, 3, 4, 4
    c1, c2, c3 = total // n1, (length + 2 * MID) // n2, (length + 80) // n3
    c4, c5 = (length + 2 * COT) // n4, length // n5
    sec_e, xh2_e, dg2_e, inv2_e = call(
        functools.partial(encoder_in, inner),
        meta,
        (rows, n1),
        [blocked(tok_ext, c1), fixed(inner_e), fixed(de), fixed(he)],
        [out_blocked(rows, total, c1, LANES, BF)] * 3 + [out_blocked(rows, total, c1, 128, F32)],
        name="encoder_in",
        flops=2 * rows * total * width * LANES,
    )
    t2 = length + 2 * MID
    out_e, xh3_e, dg3_e, inv3_e, third_e, sec_d, xh2_d, dg2_d, inv2_d = call(
        functools.partial(encoder_out, inner, c2),
        meta,
        (rows, n2),
        [
            whole_row(sec_e), element(tok_ext, c2, TOK - MID), element(masks, c2, TOK - MID),
            fixed(conv_e), fixed(outer_e), fixed(inner_d), fixed(de), fixed(he), fixed(dd), fixed(hd),
        ],
        [
            out_blocked(rows, t2, c2, width, F32),
            out_blocked(rows, t2, c2, LANES, BF), out_blocked(rows, t2, c2, LANES, BF), out_blocked(rows, t2, c2, 128, F32),
            out_blocked(rows, t2, c2, 128, BF),
            out_blocked(rows, t2, c2, LANES, BF), out_blocked(rows, t2, c2, LANES, BF),
            out_blocked(rows, t2, c2, LANES, BF), out_blocked(rows, t2, c2, 128, F32),
        ],
        [pltpu.VMEM((c2, LANES), BF)],
        name="encoder_out",
        flops=2 * rows * t2 * LANES * (5 * LANES + 2 * width),
    )
    t3 = length + 80
    final = jax.ShapeDtypeStruct((rows_all, length, width), F32)
    hbm = pl.BlockSpec(memory_space=pl.ANY)
    seed = jnp.zeros((8, 128), F32)
    mine_out, other_out, mixed_d, go_d, gc_d, gdo_d, gh3_d = call(
        functools.partial(decoder_out, inner, c3, length),
        meta,
        (rows, n3),
        [
            whole_row(sec_d), element(out_e, c3, MID - COT), blocked(cot_ext, c3), element(masks, c3, TOK - COT),
            fixed(conv_d), fixed(outer_d), fixed(dd), fixed(hd), (seed, hbm),
        ],
        [
            (final, hbm),
            (jax.ShapeDtypeStruct((rows, length, width), BF), hbm),
            out_blocked(rows, t3, c3, LANES, BF),
            out_fixed((128, width)), out_fixed((3, 128, LANES)), out_fixed((8, width)), out_fixed((24, LANES)),
        ],
        [
            pltpu.VMEM((c3, LANES), BF), pltpu.VMEM((c3, LANES), BF),
            pltpu.VMEM((rows, t3, width), F32), pltpu.VMEM((rows, t3, width), BF),
            pltpu.SemaphoreType.DMA((2, rows)),
        ],
        name="decoder_out",
        flops=2 * rows * t3 * LANES * (3 * LANES + 2 * width + 3 * 128),
    )
    t4 = length + 2 * COT
    grad_d, mixed_e, gi_d, gd_d, gh2_d, go_e, gdo_e, gh3_e = call(
        functools.partial(decoder_back, inner, c4),
        meta,
        (rows, n4),
        [
            whole_row(mixed_d), element(xh2_d, c4, MID - COT), element(dg2_d, c4, MID - COT), element(inv2_d, c4, MID - COT),
            element(out_e, c4, MID - COT), blocked(cot_ext, c4), element(masks, c4, TOK - COT),
            fixed(conv_d), fixed(inner_d), fixed(dd), fixed(hd),
            element(xh3_e, c4, MID - COT), element(dg3_e, c4, MID - COT), element(inv3_e, c4, MID - COT),
            element(third_e, c4, MID - COT), fixed(outer_e), fixed(he),
        ],
        [
            out_blocked(rows, t4, c4, width, F32), out_blocked(rows, t4, c4, LANES, BF),
            out_fixed((128, width)), out_fixed((16, width)), out_fixed((24, LANES)),
            out_fixed((128, width)), out_fixed((8, width)), out_fixed((24, LANES)),
        ],
        [pltpu.VMEM((c4, LANES), BF)],
        name="decoder_back",
        flops=2 * rows * t4 * LANES * (3 * LANES + 3 * width),
    )
    mine_grad, other_grad, gi_e, gc_e, gd_e, gh2_e = call(
        functools.partial(encoder_back, inner, c5),
        meta,
        (rows, n5),
        [
            whole_row(mixed_e), whole_row(sec_e),
            element(xh2_e, c5, TOK), element(dg2_e, c5, TOK), element(inv2_e, c5, TOK),
            element(tok_ext, c5, TOK), element(grad_d, c5, COT), element(masks, c5, TOK),
            fixed(conv_e), fixed(inner_e), fixed(de), fixed(he), (seed, hbm),
        ],
        [
            (final, pl.BlockSpec((1, c5, width), lambda r, i, m: (m[0] * rows + r, i, 0))),
            out_blocked(rows, length, c5, width, BF),
            out_fixed((128, width)), out_fixed((5, 128, LANES)), out_fixed((16, width)), out_fixed((24, LANES)),
        ],
        [pltpu.VMEM((c5, LANES), BF)],
        name="encoder_back",
        flops=2 * rows * length * LANES * (5 * LANES + 2 * width + 5 * 128),
    )

    def finish(mine, other):
        return call(
            fill_rows,
            meta,
            (rows, 4),
            [blocked(flip(other, "pipe", 1), length // 4), (mine, hbm)],
            [
                (
                    final,
                    pl.BlockSpec((1, length // 4, width), lambda r, i, m: ((1 - m[0]) * rows + r, i, 0)),
                )
            ],
            aliases={2: 0},
            name="fill_rows",
            nbytes=rows * length * width * 6,
        )[0]

    section_output = finish(mine_out, other_out)[None]
    input_gradient = finish(mine_grad, other_grad)[None]

    def pick(e, d):
        kept = jnp.where(encoder_side, e, d)
        sent = jnp.where(encoder_side, d, e)
        return kept + flip(sent.astype(BF), "pipe", 1).astype(F32)

    offset = (tensor * lanes) % 128

    def own(array):
        return lax.dynamic_slice_in_dim(array, offset, lanes, array.ndim - 2)

    inner_sum, outer_sum = pick(own(gi_e), own(gi_d)), pick(own(go_e), own(go_d))
    conv_sum = pick(own(gc_e[:4]), own(jnp.concatenate([gc_e[4:], gc_d], axis=0)))
    sizes = [inner_sum.size, outer_sum.size, conv_sum.size]
    flat = jnp.concatenate([inner_sum.reshape(-1), outer_sum.reshape(-1), conv_sum.reshape(-1)])
    unit = 128 * 16 * n_seq
    flat = pad_to(flat, 0, -(-flat.size // unit) * unit).reshape(-1, 128)
    flat = sum_over(flat, "seq").reshape(-1)
    grad_inner = jnp.transpose(flat[: sizes[0]].reshape(lanes, width)[:local])
    grad_outer = flat[sizes[0] : sizes[0] + sizes[1]].reshape(lanes, width)[:local]
    conv_sum = flat[sizes[0] + sizes[1] : sum(sizes)].reshape(4, lanes, n_tensor, lanes)
    conv_sum = conv_sum[:, :local, :, :local].reshape(4, local, inner)
    conv_sum = jnp.transpose(conv_sum, (0, 2, 1))
    conv_other = flip(conv_sum.astype(BF), "pipe", 1).astype(F32)
    conv_first = jnp.where(encoder_side, conv_sum, conv_other)
    conv_second = jnp.where(encoder_side, conv_other, conv_sum)
    grad_conv_e = jnp.concatenate([conv_first, conv_second[:1]], axis=0)
    grad_conv_d = conv_second[1:]

    def fold(array, count):
        return jnp.sum(array.reshape(count, 8, array.shape[-1]), axis=1)

    wide = pick(
        jnp.concatenate([fold(gd_e, 2), fold(gdo_e, 1)], axis=0), jnp.concatenate([fold(gd_d, 2), fold(gdo_d, 1)], axis=0)
    )
    narrow = pick(
        jnp.concatenate([fold(gh2_e, 3), fold(gh3_e, 3)], axis=0), jnp.concatenate([fold(gh2_d, 3), fold(gh3_d, 3)], axis=0)
    )
    narrow = lax.dynamic_slice_in_dim(narrow, tensor * lanes, lanes, 1)
    vectors = jnp.concatenate([wide.reshape(-1), narrow.reshape(-1)])
    count = vectors.size
    vectors = pad_to(vectors, 0, -(-count // unit) * unit).reshape(-1, 128)
    vectors = sum_over(vectors, "seq").reshape(-1)
    wide = vectors[: 3 * width].reshape(3, width)
    narrow = vectors[3 * width : count].reshape(6, lanes)[:, :local]

    return (
        section_output,
        input_gradient,
        wide[0][None],
        wide[1][None],
        grad_inner[None],
        narrow[2][None],
        narrow[0][None],
        narrow[1][None],
        grad_conv_e,
        grad_conv_d,
        narrow[5][None],
        narrow[3][None],
        narrow[4][None],
        grad_outer[None],
        wide[2][None],
    )


def solution(mesh):
    return jax.shard_map(
        on_device,
        mesh=mesh,
        in_specs=(
            P(None, "seq", None),
            P(None, "seq"),
            P(None, "seq"),
            P(None, "seq", None),
            P("pipe", None),
            P("pipe", None),
            P("pipe", None, "tensor"),
            P("pipe", "tensor"),
            P("pipe", "tensor"),
            P("pipe", "tensor"),
            P(None, None, "tensor"),
            P(None, None, "tensor"),
            P("pipe", "tensor"),
            P("pipe", "tensor"),
            P("pipe", "tensor"),
            P("pipe", "tensor", None),
            P("pipe", None),
        ),
        out_specs=(
            P("pipe", None, "seq", None),
            P("pipe", None, "seq", None),
            P("pipe", None),
            P("pipe", None),
            P("pipe", None, "tensor"),
            P("pipe", "tensor"),
            P("pipe", "tensor"),
            P("pipe", "tensor"),
            P(None, None, "tensor"),
            P(None, None, "tensor"),
            P("pipe", "tensor"),
            P("pipe", "tensor"),
            P("pipe", "tensor"),
            P("pipe", "tensor", None),
            P("pipe", None),
        ),
        check_vma=False,
    )
```

```python
import functools
import math

import jax
import jax.numpy as jnp
from jax import lax
from jax.experimental import pallas as pl
from jax.experimental.pallas import tpu as pltpu
from jax.sharding import PartitionSpec as P

SPACING = 16
EPSILON = 1e-05
BF = jnp.bfloat16
F32 = jnp.float32
LANES = 512
TILE = 128
CHUNK = 256
BLOCK = 16
PIECE = 208
ROOT = math.sqrt(2.0 / math.pi)
CUBIC = 0.044715
E_OFFSETS = tuple(SPACING * (k - 2) for k in range(5))
D_OFFSETS = (-2, -1, 0)
VMEM = 60 * 1024 * 1024
FREE = 120
COT_TURNS = (96, 48)


def dot(a, b):
    return lax.dot_general(a, b, (((1,), (0,)), ((), ())), preferred_element_type=F32)


def dot_nt(a, b):
    return lax.dot_general(a, b, (((1,), (1,)), ((), ())), preferred_element_type=F32)


def pair(column):
    return jnp.concatenate([column, column], axis=1)


def row_sum(values):
    return jnp.sum(values, axis=0, keepdims=True)


def moments(get, count):
    total = square = None
    for j in range(0, count, BLOCK):
        x = get(j)
        total = x if total is None else total + x
        square = x * x if square is None else square + x * x
    center = row_sum(total) * (1.0 / count)
    inverse = lax.rsqrt(row_sum(square) * (1.0 / count) - center * center + EPSILON)
    return center * inverse, inverse


def gate(half):
    square = half * half
    return jnp.tanh(half * (2 * ROOT + (8 * CUBIC * ROOT) * square)), square


def slope(half, tanh, square):
    return (1.0 + tanh) * (0.5 + (half - half * tanh) * (ROOT + (12 * CUBIC * ROOT) * square))


def spread(target, source, columns, *whole):
    for n, c in enumerate(columns):
        value = jnp.broadcast_to(source[:, c : c + 1], target.shape[1:])
        target[n] = value if n in [w - 1 for w in whole] else 0.5 * value


def param(ref, n, j):
    return pair(ref[n, j : j + BLOCK, :])


def placed(sel, a_ref, b_ref, lo):
    parts = []
    for q in range(a_ref.shape[0]):
        part = jnp.where(sel, a_ref[q, lo : lo + PIECE, :], b_ref[q, lo : lo + PIECE, :])
        parts.append(part.astype(F32)[:200])
    return jnp.concatenate(parts, axis=0).astype(BF)


def tap_of(sel, a_ref, b_ref, tap, inner):
    q = tap % 4
    first, second = a_ref[q, :inner, :], b_ref[q, :inner, :]
    return jnp.where(sel, first, second) if tap < 4 else jnp.where(sel, second, first)


def drive(streams):
    streams = list(streams)
    while streams:
        for stream in tuple(streams):
            try:
                next(stream)
            except StopIteration:
                streams.remove(stream)


def tiles_of(step):
    return jnp.where(step == 0, 1, 2 * step), jnp.where(step == 0, 10, 2 * step + 1)


def at_tile(a, count=1):
    return pl.ds(pl.multiple_of(a * TILE, TILE), count * TILE)


def code_rows(code_ref, n, a, offsets):
    window = code_ref[n, :, at_tile(a - 1, 3)]
    here = window[:, TILE : 2 * TILE]
    return [(window[:, TILE + o : 2 * TILE + o] == here).astype(F32) for o in offsets], (here > 0.5).astype(F32)


def taps(cat_ref, ref, code_ref, n, step, offsets, count):
    kept = []
    for half, a in enumerate(tiles_of(step)):
        masks, keep = code_rows(code_ref, n, a, offsets)
        kept.append(keep)
        lanes = slice(n * CHUNK + half * TILE, n * CHUNK + (half + 1) * TILE)
        window = ref[n, :, at_tile(a - 1, 3)]
        for k, offset in enumerate(offsets):
            piece = window[:, TILE + offset : 2 * TILE + offset]
            if offset:
                piece = piece * masks[k].astype(BF)
            cat_ref[k * count : (k + 1) * count, lanes] = piece
    return jnp.concatenate(kept, axis=1)


def row_taps(cat_ref, ref, col_ref, n, step, offsets):
    for half, a in enumerate(tiles_of(step)):
        here = col_ref[n, at_tile(a), :]
        rows = slice(n * CHUNK + half * TILE, n * CHUNK + (half + 1) * TILE)
        for k, offset in enumerate(offsets):
            there = pl.ds(pl.multiple_of(a * TILE + offset, BLOCK), TILE)
            piece = ref[n, there, :]
            if offset:
                mask = (col_ref[n, there, :] == here).astype(BF)
                piece = piece * jnp.concatenate([mask] * (LANES // TILE), axis=1)
            cat_ref[rows, k * LANES : (k + 1) * LANES] = piece


def put_rows(ext_ref, n, step, values):
    turned = jnp.transpose(values[...])
    for half, a in enumerate(tiles_of(step)):
        ext_ref[n, at_tile(a), 0 : turned.shape[1]] = turned[half * TILE : (half + 1) * TILE, :]


def keep_row(code_ref, n, step):
    return jnp.concatenate([(code_ref[n, :, at_tile(a)] > 0.5).astype(F32) for a in tiles_of(step)], axis=1)


def put(ext_ref, n, step, values):
    for half, a in enumerate(tiles_of(step)):
        ext_ref[n, :, at_tile(a)] = values[:, half * TILE : (half + 1) * TILE]


def blank_ends(ext_ref):
    for a in (0, 11):
        ext_ref[:, :, a * TILE : (a + 1) * TILE] = jnp.zeros(ext_ref.shape[:2] + (TILE,), BF)


def from_sums(total, square, count):
    center = row_sum(total) * (1.0 / count)
    inverse = lax.rsqrt(row_sum(square) * (1.0 / count) - center * center + EPSILON)
    return center * inverse, inverse


def biased(hid_ref, product, ph, n):
    count = hid_ref.shape[0]
    total = square = None
    for j in range(0, count, BLOCK):
        x = product[j : j + BLOCK, :] + param(ph, n, j)
        hid_ref[j : j + BLOCK, :] = x
        total = x if total is None else total + x
        square = x * x if square is None else square + x * x
    return from_sums(total, square, count)


def activate(hid_ref, stats, ph, gain, bias, out_ref, xh_ref, dg_ref, inv_ref):
    shift, inverse = stats
    inv_ref[...] = jnp.broadcast_to(inverse, inv_ref.shape)
    for j in range(0, hid_ref.shape[0], BLOCK):
        scaled = hid_ref[j : j + BLOCK, :] * inverse - shift
        half = scaled * param(ph, gain, j) + param(ph, bias, j)
        tanh, square = gate(half)
        out_ref[j : j + BLOCK, :] = (half + half * tanh).astype(BF)
        xh_ref[j : j + BLOCK, :] = scaled.astype(BF)
        dg_ref[j : j + BLOCK, :] = slope(half, tanh, square).astype(BF)


def first_of(x_ref, stats, pd, gain, out_ref, slope_ref=None):
    shift, inverse = stats
    for j in range(0, x_ref.shape[0], BLOCK):
        scaled = x_ref[j : j + BLOCK, :] * inverse - shift
        half = scaled * param(pd, gain, j) + param(pd, gain + 1, j)
        tanh, square = gate(half)
        out_ref[j : j + BLOCK, :] = (half + half * tanh).astype(BF)
        if slope_ref is not None:
            slope_ref[j : j + BLOCK, :] = slope(half, tanh, square)


def moments_of(x_ref):
    return moments(lambda j: x_ref[j : j + BLOCK, :], x_ref.shape[0])


def halves(values):
    return values[:, :TILE] + values[:, TILE:]


def norm_back(grad, xh_ref, dg_ref, inverse, ph, gain, low_ref, wide_ref, acc, base):
    count = low_ref.shape[0]
    first = second = None
    for j in range(0, count, BLOCK):
        down = grad[j : j + BLOCK, :] * dg_ref[j : j + BLOCK, :].astype(F32)
        cross = down * xh_ref[j : j + BLOCK, :].astype(F32)
        acc[base, j : j + BLOCK, :] += halves(cross)
        acc[base + 1, j : j + BLOCK, :] += halves(down)
        g = param(ph, gain, j)
        weighted = down * g
        wide_ref[j : j + BLOCK, :] = weighted
        first = weighted if first is None else first + weighted
        second = cross * g if second is None else second + cross * g
    twice = inverse * 2.0
    first = row_sum(first) * (twice * (1.0 / count))
    second = row_sum(second) * (twice * (1.0 / count))
    for j in range(0, count, BLOCK):
        result = wide_ref[j : j + BLOCK, :] * twice - first - xh_ref[j : j + BLOCK, :].astype(F32) * second
        low_ref[j : j + BLOCK, :] = result.astype(BF)
        acc[base + 2, j : j + BLOCK, :] += halves(result)


def own_rows(pick_ref, values):
    return dot(pick_ref[...], values).astype(BF)


def columns(target, lane, acc, order):
    count = acc.shape[1]
    for n, k in enumerate(order):
        target[0:count, lane + n : lane + n + 1] = jnp.sum(acc[k], axis=1, keepdims=True)


def clear(step, *refs):
    @pl.when(step <= 1)
    def _():
        for ref in refs:
            ref[...] = jnp.zeros_like(ref)


def turned(tile, by):
    return pltpu.roll(tile, by, 1) if by else tile


def fetch(step, target, own_ref, before_ref, after_ref, turns):
    @pl.when(step == 0)
    def _():
        width = target.shape[1]
        for n in range(2):
            target[n, :, 0:TILE] = turned(before_ref[n, 0:width, :].astype(F32), turns[0])
            target[n, :, TILE:] = turned(after_ref[n, 0:width, :].astype(F32), turns[1])

    @pl.when(step > 0)
    def _():
        target[...] = own_ref[...]


def encoder_in(meta, tok_ref, before_ref, after_ref, a_ref, b_ref, eye_ref, pd_ref, ph_ref,
               sec_ref, xh_ref, dg_ref, inv_ref, wi, pd, ph, x_s, first_s, hid_s, sec_s):
    step = pl.program_id(0)

    @pl.when(step == 0)
    def _():
        spread(pd, pd_ref, (0, 1))
        spread(ph, ph_ref, (0, 1, 2), 1)
        wi[...] = dot_nt(eye_ref[...], placed(meta[0] == 0, a_ref, b_ref, 0)).astype(BF)
        sec_ref[...] = jnp.zeros_like(sec_ref)

    fetch(step, x_s, tok_ref, before_ref, after_ref, (0, 0))

    def stream(n):
        first_of(x_s.at[n], moments_of(x_s.at[n]), pd, 0, first_s.at[n])
        product = dot(wi[...], first_s[n])
        yield
        stats = biased(hid_s.at[n], product, ph, 0)
        activate(hid_s.at[n], stats, ph, 1, 2, sec_s.at[n], xh_ref.at[n], dg_ref.at[n], inv_ref.at[n])
        put_rows(sec_ref, n, step, sec_s.at[n])

    drive(stream(n) for n in range(2))


def encoder_out(meta, sec_ref, code_ref, col_ref, tok_ref, before_ref, after_ref, a_ref, b_ref, ao_ref, bo_ref, ai_ref, bi_ref,
                eye_ref, pick_ref, pd_ref, ph_ref,
                out_ref, xh3_ref, dg3_ref, inv3_ref, third_ref, secd_ref, xh2_ref, dg2_ref, inv2_ref,
                wc, wo, wi, pd, ph, cat, hid_s, third_s, first_s, sec_s):
    step = pl.program_id(0)
    width = tok_ref.shape[1]
    inner = eye_ref.shape[0]

    @pl.when(step == 0)
    def _():
        spread(pd, pd_ref, (2, 3, 4), 1)
        spread(ph, ph_ref, (3, 4, 5, 6, 7, 8), 1, 4)
        sel = meta[0] == 0
        wc[...] = jnp.zeros_like(wc)
        for k in range(5):
            wc[:, k * LANES : k * LANES + inner] = dot_nt(eye_ref[...], tap_of(sel, a_ref, b_ref, k, inner)).astype(BF)
        wo[...] = dot_nt(placed(sel, ao_ref, bo_ref, 0), eye_ref[...]).astype(BF)
        wi[...] = dot_nt(eye_ref[...], placed(sel, bi_ref, ai_ref, 0)).astype(BF)
        blank_ends(secd_ref)

    fetch(step, out_ref, tok_ref, before_ref, after_ref, (0, 0))

    def stream(n):
        row_taps(cat, sec_ref, col_ref, n, step, E_OFFSETS)
        keep = keep_row(code_ref, n, step)
        product = dot_nt(wc[...], cat[n * CHUNK : (n + 1) * CHUNK, :])
        yield
        stats = biased(hid_s.at[n], product, ph, 0)
        activate(hid_s.at[n], stats, ph, 1, 2, third_s.at[n], xh3_ref.at[n], dg3_ref.at[n], inv3_ref.at[n])
        product = dot(wo[...], third_s[n])
        third_ref[n] = own_rows(pick_ref, third_s[n])
        yield
        kept = jnp.broadcast_to(keep, (BLOCK, CHUNK))
        total = square = None
        for j in range(0, width, BLOCK):
            x = out_ref[n, j : j + BLOCK, :] + kept * (product[j : j + BLOCK, :] + param(pd, 0, j))
            out_ref[n, j : j + BLOCK, :] = x
            total = x if total is None else total + x
            square = x * x if square is None else square + x * x
        first_of(out_ref.at[n], from_sums(total, square, width), pd, 1, first_s.at[n])
        product = dot(wi[...], first_s[n])
        yield
        stats = biased(hid_s.at[n], product, ph, 3)
        activate(hid_s.at[n], stats, ph, 4, 5, sec_s.at[n], xh2_ref.at[n], dg2_ref.at[n], inv2_ref.at[n])
        put(secd_ref, n, step, sec_s.at[n])

    drive(stream(n) for n in range(2))


def decoder_out(meta, sec_ref, code_ref, in_ref, cot_ref, before_ref, after_ref, a_ref, b_ref, ao_ref, bo_ref, eye_ref, pick_ref,
                pd_ref, ph_ref,
                mine_ref, other_ref, mixed_ref, go_ref, gc_ref,
                wc, wo, wob, pd, ph, cat, hid_s, third_s, cot_f, cot_s, low_s, xh_s, dg_s, inv_s, accd, acch):
    step = pl.program_id(0)
    width = in_ref.shape[1]
    inner = eye_ref.shape[0]

    @pl.when(step == 0)
    def _():
        spread(pd, pd_ref, (5,), 1)
        spread(ph, ph_ref, (9, 10, 11), 1)
        sel = meta[0] == 0
        for k in range(3):
            wc[:, k * inner : (k + 1) * inner] = dot_nt(eye_ref[...], tap_of(sel, a_ref, b_ref, 5 + k, inner)).astype(BF)
        outer = placed(sel, bo_ref, ao_ref, 0)
        wo[...] = dot_nt(outer, eye_ref[...]).astype(BF)
        wob[...] = dot_nt(eye_ref[...], outer).astype(BF)
        blank_ends(mixed_ref)

    clear(step, go_ref, gc_ref, accd, acch)
    fetch(step, cot_f, cot_ref, before_ref, after_ref, COT_TURNS)
    encoder_side = meta[0] == 0

    def stream(n):
        lanes = slice(n * CHUNK, (n + 1) * CHUNK)
        kept = jnp.broadcast_to(keep_row(code_ref, n, step), (BLOCK, CHUNK))
        for j in range(0, width, BLOCK):
            branch = kept * cot_f[n, j : j + BLOCK, :]
            accd[0, j : j + BLOCK, :] += halves(branch)
            cot_s[j : j + BLOCK, lanes] = branch.astype(BF)
        taps(cat, sec_ref, code_ref, n, step, D_OFFSETS, inner)
        product = dot(wc[...], cat[:, lanes])
        grad = dot(wob[...], cot_s[:, lanes])
        yield
        stats = biased(hid_s.at[n], product, ph, 0)
        activate(hid_s.at[n], stats, ph, 1, 2, third_s.at[n], xh_s.at[n], dg_s.at[n], inv_s.at[n])
        product = dot(wo[...], third_s[n])
        norm_back(grad, xh_s.at[n], dg_s.at[n], stats[1], ph, 1, low_s.at[n], hid_s.at[n], acch, 0)
        put(mixed_ref, n, step, low_s.at[n])
        yield
        for j in range(0, width, BLOCK):
            x = in_ref[n, j : j + BLOCK, :]
            y = x + kept * (product[j : j + BLOCK, :] + param(pd, 0, j))
            mine_ref[n, j : j + BLOCK, :] = jnp.where(encoder_side, x, y)
            other_ref[n, j : j + BLOCK, :] = jnp.where(encoder_side, y, x).astype(BF)

    drive(stream(n) for n in range(2))
    picked = own_rows(pick_ref, jnp.concatenate([third_s[0], third_s[1], low_s[0], low_s[1]], axis=1))
    go_ref[...] += dot_nt(cot_s[...], picked[:, : 2 * CHUNK])
    gc_ref[...] += dot_nt(cat[...], picked[:, 2 * CHUNK :])

    @pl.when(step == 4)
    def _():
        columns(go_ref, FREE, accd, (0,))
        columns(go_ref, FREE + 1, acch, (0, 1, 2))


def inner_back(n, grad_second, xh2_ref, dg2_ref, inv2_ref, in_ref, wib, pd, ph, hid_s, low_s, first_s, dg1_s, acch, accd, finish):
    lanes = slice(n * CHUNK, (n + 1) * CHUNK)
    width = in_ref.shape[1]
    stats = shift, inverse = moments_of(in_ref.at[n])
    first_of(in_ref.at[n], stats, pd, 0, first_s.at[:, lanes], dg1_s.at[n])
    norm_back(grad_second, xh2_ref.at[n], dg2_ref.at[n], inv2_ref[n, 0:1, :], ph, 0, low_s.at[n], hid_s.at[n], acch, 0)
    grad = dot(wib[...], low_s[n])
    yield
    first = second = None
    for j in range(0, width, BLOCK):
        scaled = in_ref[n, j : j + BLOCK, :] * inverse - shift
        down = grad[j : j + BLOCK, :] * dg1_s[n, j : j + BLOCK, :]
        cross = down * scaled
        accd[0, j : j + BLOCK, :] += halves(cross)
        accd[1, j : j + BLOCK, :] += halves(down)
        g = param(pd, 0, j)
        weighted = down * g
        dg1_s[n, j : j + BLOCK, :] = weighted
        first = weighted if first is None else first + weighted
        second = cross * g if second is None else second + cross * g
    twice = inverse * 2.0
    first = row_sum(first) * (twice * (1.0 / width))
    second = row_sum(second) * (twice * (1.0 / width))
    for j in range(0, width, BLOCK):
        scaled = in_ref[n, j : j + BLOCK, :] * inverse - shift
        finish(j, dg1_s[n, j : j + BLOCK, :] * twice - first - scaled * second)


def decoder_back(meta, mixed_ref, code_ref, xh2_ref, dg2_ref, inv2_ref, in_ref, cot_ref, before_ref, after_ref,
                 xh3_ref, dg3_ref, inv3_ref, third_ref, a_ref, b_ref, ai_ref, bi_ref, ao_ref, bo_ref, eye_ref, pick_ref,
                 pd_ref, ph_ref,
                 grad_ref, low3_ref, gi_ref, go_ref,
                 wc, wib, wob, pd, ph, cat, hid_s, low_s, low3_s, first_s, branch_s, dg1_s, accd, acch):
    step = pl.program_id(0)
    inner = eye_ref.shape[0]

    @pl.when(step == 0)
    def _():
        spread(pd, pd_ref, (3, 4))
        spread(ph, ph_ref, (7, 4))
        sel = meta[0] == 0
        for k in range(3):
            wc[:, k * inner : (k + 1) * inner] = dot_nt(tap_of(sel, a_ref, b_ref, 5 + k, inner), eye_ref[...]).astype(BF)
        wib[...] = dot_nt(placed(sel, bi_ref, ai_ref, 0), eye_ref[...]).astype(BF)
        wob[...] = dot_nt(eye_ref[...], placed(sel, ao_ref, bo_ref, 0)).astype(BF)
        low3_ref[...] = jnp.zeros_like(low3_ref)

    clear(step, gi_ref, go_ref, accd, acch)
    fetch(step, grad_ref, cot_ref, before_ref, after_ref, COT_TURNS)

    def stream(n):
        lanes = slice(n * CHUNK, (n + 1) * CHUNK)
        keep = taps(cat, mixed_ref, code_ref, n, step, tuple(-o for o in D_OFFSETS), inner)
        kept = jnp.broadcast_to(keep, (BLOCK, CHUNK))
        grad = dot(wc[...], cat[:, lanes])
        yield

        def finish(j, value):
            value = grad_ref[n, j : j + BLOCK, :] + value
            grad_ref[n, j : j + BLOCK, :] = value
            branch = kept * value
            accd[2, j : j + BLOCK, :] += halves(branch)
            branch_s[j : j + BLOCK, lanes] = branch.astype(BF)

        yield from inner_back(
            n, grad, xh2_ref, dg2_ref, inv2_ref, in_ref, wib, pd, ph, hid_s, low_s, first_s, dg1_s, acch, accd, finish
        )
        grad = dot(wob[...], branch_s[:, lanes])
        yield
        norm_back(grad, xh3_ref.at[n], dg3_ref.at[n], inv3_ref[n, 0:1, :], ph, 1, low3_s.at[n], hid_s.at[n], acch, 3)
        put_rows(low3_ref, n, step, low3_s.at[n])

    drive(stream(n) for n in range(2))
    low = own_rows(pick_ref, jnp.concatenate([low_s[0], low_s[1]], axis=1))
    third = jnp.concatenate([third_ref[n] for n in range(2)], axis=1)
    gi_ref[...] += dot_nt(first_s[...], low)
    go_ref[...] += dot_nt(branch_s[...], third)

    @pl.when(step == 4)
    def _():
        columns(gi_ref, FREE, accd, (0, 1))
        columns(gi_ref, FREE + 2, acch, (0, 1, 2))
        columns(go_ref, FREE, accd, (2,))
        columns(go_ref, FREE + 1, acch, (3, 4, 5))


def encoder_back(meta, mixed_ref, sec_ref, col_ref, xh2_ref, dg2_ref, inv2_ref, in_ref, later_ref, a_ref, b_ref,
                 ai_ref, bi_ref, eye_ref, pick_ref, pd_ref, ph_ref,
                 mine_ref, other_ref, gi_ref, gc_ref,
                 wc, wib, pd, ph, cat, catw, gc_s, hid_s, low_s, first_s, dg1_s, accd, acch):
    step = pl.program_id(0) + 1
    inner = eye_ref.shape[0]

    @pl.when(step == 1)
    def _():
        spread(pd, pd_ref, (0, 1))
        spread(ph, ph_ref, (1,))
        sel = meta[0] == 0
        wc[...] = jnp.zeros_like(wc)
        for k in range(5):
            wc[:, k * LANES : k * LANES + inner] = dot_nt(tap_of(sel, a_ref, b_ref, k, inner), eye_ref[...]).astype(BF)
        wib[...] = dot_nt(placed(sel, ai_ref, bi_ref, 0), eye_ref[...]).astype(BF)

    clear(step, gi_ref, gc_s, accd, acch)
    encoder_side = meta[0] == 0

    def stream(n):
        lanes = slice(n * CHUNK, (n + 1) * CHUNK)
        row_taps(cat, mixed_ref, col_ref, n, step, tuple(-o for o in E_OFFSETS))
        grad = dot_nt(wc[...], cat[lanes, :])
        yield

        def finish(j, value):
            later = later_ref[n, j : j + BLOCK, :]
            value = later + value
            mine_ref[n, j : j + BLOCK, :] = jnp.where(encoder_side, value, later)
            other_ref[n, j : j + BLOCK, :] = jnp.where(encoder_side, later, value).astype(BF)

        yield from inner_back(
            n, grad, xh2_ref, dg2_ref, inv2_ref, in_ref, wib, pd, ph, hid_s, low_s, first_s, dg1_s, acch, accd, finish
        )
        row_taps(catw, sec_ref, col_ref, n, step, E_OFFSETS)

    drive(stream(n) for n in range(2))
    low = own_rows(pick_ref, jnp.concatenate([low_s[0], low_s[1]], axis=1))
    mixed = jnp.concatenate(
        [dot_nt(pick_ref[...], mixed_ref[n, at_tile(2 * step, 2), 0:inner]).astype(BF) for n in range(2)], axis=1
    )
    gi_ref[...] += dot_nt(first_s[...], low)
    gc_s[...] += dot(mixed, catw[...])

    @pl.when(step == 4)
    def _():
        columns(gi_ref, FREE, accd, (0, 1))
        columns(gi_ref, FREE + 2, acch, (0, 1, 2))
        for k in range(5):
            gc_ref[k * inner : (k + 1) * inner, :] = jnp.transpose(gc_s[:, k * LANES : k * LANES + inner])


def fill_rows(meta, recv_ref, final_ref, out_ref):
    del meta, final_ref
    out_ref[...] = recv_ref[...].astype(F32)


def pack_edges(meta, tok_last, cot_last, tok_first, cot_first, code_last, code_first, tail_ref, head_ref):
    del meta
    width = tok_last.shape[1]
    lane = lax.broadcasted_iota(jnp.int32, (width, TILE), 1)
    for n in range(2):
        tail_ref[n, 0:width, :] = jnp.where(lane < 32, turned(cot_last[n], 32), tok_last[n]).astype(BF)
        head_ref[n, 0:width, :] = jnp.where(lane < 80, tok_first[n], turned(cot_first[n], 80)).astype(BF)
        tail_ref[n, width:, :] = jnp.broadcast_to(code_last[n], (BLOCK, TILE)).astype(BF)
        head_ref[n, width:, :] = jnp.broadcast_to(code_first[n], (BLOCK, TILE)).astype(BF)


def place_weights(place, own_ref, *refs):
    out_ref = refs[-1]
    for q in range(4):
        out_ref[q, :, at_tile(place[1])] = own_ref[q]
    for by in range(4):
        for slot in range(1, 4):
            out_ref[place[0] ^ by, :, at_tile(place[1] ^ slot)] = refs[by][slot - 1]


def pack_grads(meta, gie, goe, gce, gid, god, gcd, kept_ref, sent_ref):
    encoder_side = meta[0] == 0
    width, most = gie.shape[0], 4 * (gce.shape[0] // 5)
    pieces = [(gie[...], gid[...]), (goe[...], god[...])]
    pieces.append((gce[0:most, :], jnp.concatenate([gce[most:, :], gcd[...]], axis=0)))
    start = 0
    for e, d in pieces:
        rows = slice(start, start + e.shape[0])
        start += e.shape[0]
        kept_ref[rows, :] = jnp.where(encoder_side, e, d)
        sent_ref[rows, :] = jnp.where(encoder_side, d, e).astype(BF)


def call(body, meta, grid, ins, outs, scratch=(), aliases=None, name=None, us=3):
    return pl.pallas_call(
        body,
        grid_spec=pltpu.PrefetchScalarGridSpec(
            num_scalar_prefetch=1,
            grid=grid,
            in_specs=[s for _, s in ins],
            out_specs=[s for _, s in outs],
            scratch_shapes=list(scratch),
        ),
        out_shape=[s for s, _ in outs],
        input_output_aliases=aliases or {},
        compiler_params=pltpu.CompilerParams(
            dimension_semantics=("arbitrary",) * len(grid), vmem_limit_bytes=VMEM
        ),
        cost_estimate=pl.CostEstimate(flops=int(us * 1.0e9), bytes_accessed=int(us * 3.5e6), transcendentals=0),
        name=name,
    )(meta, *[a for a, _ in ins])


def per_step(array, steps=5):
    first = array.shape[0] // 2 - steps
    return (array, pl.BlockSpec((2,) + array.shape[1:], lambda c, m: (c + first, 0, 0)))


def own_index(c, m):
    return (m[0], 0, jnp.maximum(c - 1, 0))


def rows_chunk(array):
    return (array, pl.BlockSpec((2, array.shape[1], CHUNK), own_index))


def fixed(array):
    zeros = (0,) * array.ndim
    return (array, pl.BlockSpec(array.shape, lambda c, m: zeros))


def part(array, rows, index):
    return (array, pl.BlockSpec((array.shape[0], rows, array.shape[2]), lambda c, m: (0, index, 0)))


def out_chunks(rows, dtype):
    return (jax.ShapeDtypeStruct((10, rows, CHUNK), dtype), pl.BlockSpec((2, rows, CHUNK), lambda c, m: (c, 0, 0)))


def out_fixed(shape, dtype=F32):
    zeros = (0,) * len(shape)
    return (jax.ShapeDtypeStruct(shape, dtype), pl.BlockSpec(shape, lambda c, m: zeros))


def flip(x, axis, by):
    count = lax.axis_size(axis)
    return lax.ppermute(x, axis, [(i, i ^ by) for i in range(count)])


def gather(x, axis):
    me = lax.axis_index(axis)
    count = lax.axis_size(axis)
    result = jnp.zeros((count,) + x.shape, x.dtype)
    result = lax.dynamic_update_index_in_dim(result, x, me, 0)
    for by in range(1, count):
        result = lax.dynamic_update_index_in_dim(result, flip(x, axis, by), me ^ by, 0)
    return result


def gather_lanes(x, axis):
    me = lax.axis_index(axis)
    count = lax.axis_size(axis)
    lanes = x.shape[-1]
    result = jnp.zeros(x.shape[:-1] + (count * lanes,), x.dtype)
    result = lax.dynamic_update_slice_in_dim(result, x, me * lanes, 1)
    for by in range(1, count):
        result = lax.dynamic_update_slice_in_dim(result, flip(x, axis, by), (me ^ by) * lanes, 1)
    return result


def spread_over(x, axis, beside):
    count = lax.axis_size(axis)
    me = lax.axis_index(axis)
    parts = x.reshape((count, x.shape[0] // count) + x.shape[1:])
    low = parts.astype(BF)
    arrived = [
        flip(lax.dynamic_index_in_dim(low, me ^ by, 0, keepdims=False), axis, by) for by in range(1, count)
    ]
    arrived, beside = lax.optimization_barrier((arrived, beside))
    total = lax.dynamic_index_in_dim(parts, me, 0, keepdims=False)
    for part_of in arrived:
        total = total + part_of.astype(F32)
    return total.astype(BF), beside


def collect_over(x, axis, beside):
    me = lax.axis_index(axis)
    count = lax.axis_size(axis)
    arrived = [flip(x, axis, by) for by in range(1, count)]
    arrived, beside = lax.optimization_barrier((arrived, beside))
    result = jnp.zeros((count,) + x.shape, x.dtype)
    result = lax.dynamic_update_index_in_dim(result, x, me, 0)
    for by in range(1, count):
        result = lax.dynamic_update_index_in_dim(result, arrived[by - 1], me ^ by, 0)
    return result.reshape((count * x.shape[0],) + x.shape[1:]), beside


def pad_to(x, axis, size):
    widths = [(0, 0)] * x.ndim
    widths[axis] = (0, size - x.shape[axis])
    return jnp.pad(x, widths)


def on_device(
    tokens, segments, pad_mask, cotangent, gain_first, bias_first, weight_inner, bias_inner, gain_middle, bias_middle,
    weight_conv_encoder, weight_conv_decoder, bias_conv, gain_last, bias_last, weight_outer, bias_outer,
):
    pipe, seq, tensor = (lax.axis_index(a) for a in ("pipe", "seq", "tensor"))
    n_pipe, n_seq, n_tensor = (lax.axis_size(a) for a in ("pipe", "seq", "tensor"))
    rows_all, length, width = tokens.shape
    rows = rows_all // n_pipe
    loc = weight_conv_encoder.shape[2]
    inner = weight_conv_encoder.shape[1]
    lanes = LANES // n_tensor
    encoder_side = pipe == 0
    meta = jnp.stack([pipe, tensor * loc]).astype(jnp.int32)
    tokens_t, cotangent_t = jnp.transpose(tokens, (0, 2, 1)), jnp.transpose(cotangent, (0, 2, 1))

    def mine_rows(array):
        return lax.dynamic_slice_in_dim(array, pipe * rows, rows, 0)

    codes = (mine_rows(jnp.where(pad_mask == 1, segments + 1, 0)).astype(F32) + 1.0)[:, None, :]
    last = length // TILE - 1

    def edge_tile(array, row, index):
        return (array, pl.BlockSpec((2, array.shape[1], TILE), lambda c, m: (m[0] if row else 0, 0, index)))

    edge_out = out_fixed((rows, width + BLOCK, TILE), BF)
    tail, head = call(
        pack_edges, meta, (1,),
        [
            edge_tile(tokens_t, True, last), edge_tile(cotangent_t, True, last),
            edge_tile(tokens_t, True, 0), edge_tile(cotangent_t, True, 0),
            edge_tile(codes, False, last), edge_tile(codes, False, 0),
        ],
        [edge_out, edge_out], name="pack_edges", us=4,
    )

    small = jnp.stack([bias_inner[0], gain_middle[0], bias_middle[0], bias_conv[0], gain_last[0], bias_last[0]])
    high = lax.reduce_precision(small, 8, 7)
    small = pad_to(jnp.concatenate([high, small - high], axis=0), 0, BLOCK)
    inner_all = pad_to(weight_inner[0].reshape(n_seq, width // n_seq, loc), 1, PIECE)
    inner_all = jnp.concatenate([inner_all, jnp.broadcast_to(small[None], (n_seq,) + small.shape)], axis=1)
    outer_all = pad_to(jnp.transpose(weight_outer[0]).reshape(n_seq, width // n_seq, loc), 1, PIECE)
    conv_all = pad_to(
        jnp.where(
            encoder_side,
            weight_conv_encoder[:4],
            jnp.concatenate([weight_conv_encoder[4:], weight_conv_decoder], axis=0),
        ), 1, 2 * PIECE,
    )

    def gathered(pieces):
        pieces = pad_to(pieces.astype(BF), 2, lanes)
        sent = lax.dynamic_index_in_dim(pieces, seq, 0, keepdims=False)
        if lanes != TILE or n_seq != 4:
            return gather(gather_lanes(sent, "tensor"), "seq")
        near = jnp.stack([flip(sent, "tensor", by) for by in range(1, 4)])
        return [pieces, near] + [flip(near, "seq", by) for by in range(1, 4)]

    def placed_parts(parts):
        if not isinstance(parts, list):
            return parts
        rows_in = parts[0].shape[1]
        return call(
            place_weights, jnp.stack([seq, tensor]).astype(jnp.int32), (1,), [fixed(x) for x in parts],
            [out_fixed((4, rows_in, LANES), BF)], name="place_weights", us=4,
        )[0]

    parts2 = gathered(jnp.concatenate([conv_all, outer_all], axis=1))
    bundle1 = placed_parts(gathered(inner_all))
    before = lax.ppermute(tail, "seq", [(i, i + 1) for i in range(n_seq - 1)])
    after = lax.ppermute(head, "seq", [(i + 1, i) for i in range(n_seq - 1)])
    large = jnp.stack([gain_first[0], bias_first[0], bias_outer[0]], axis=0)
    bundle1b, large2 = flip(bundle1, "pipe", 1), flip(large, "pipe", 1)
    def columns_of(mine, other):
        first, second = jnp.where(encoder_side, mine, other), jnp.where(encoder_side, other, mine)
        return pad_to(jnp.transpose(jnp.concatenate([first, second], axis=0)), 1, TILE)

    def small_of(bundle):
        values = bundle[0, PIECE : PIECE + 12].astype(F32)
        values = (values[:6] + values[6:]).reshape(6, n_tensor, lanes)
        return values[:, :, :loc].reshape(6, inner)

    ph, pd = columns_of(small_of(bundle1), small_of(bundle1b)), columns_of(large, large2)
    first_lane = jnp.arange(inner)
    first_lane = first_lane // loc * lanes + first_lane % loc
    eye = (first_lane[:, None] == jnp.arange(LANES)[None, :]).astype(BF)
    own = (jnp.arange(TILE)[:, None] + tensor * loc == jnp.arange(inner)[None, :]) & (jnp.arange(TILE)[:, None] < loc)
    own = own.astype(BF)
    w_inner = [part(bundle1, PIECE + BLOCK, 0), part(bundle1b, PIECE + BLOCK, 0)]
    none = jnp.zeros((rows, 1, TILE), F32)
    codes = jnp.concatenate(
        [none, before[:, width : width + 1].astype(F32), codes, after[:, width : width + 1].astype(F32), none], axis=2
    ) - 1.0
    code_cols = jnp.broadcast_to(codes[:, 0, :, None], (rows, codes.shape[2], TILE)).astype(BF)
    halo = [fixed(before), fixed(after)]

    ext = length + 4 * TILE
    scr = pltpu.VMEM
    chunk_f = scr((2, width, CHUNK), F32)
    chunk_b = scr((2, width, CHUNK), BF)
    both_b = scr((width, 2 * CHUNK), BF)
    hid_f = scr((2, inner, CHUNK), F32)
    hid_b = scr((2, inner, CHUNK), BF)

    def pds(n):
        return scr((n, width, TILE), F32)

    def phs(n):
        return scr((n, inner, TILE), F32)

    last_ins = [fixed(eye), fixed(own), fixed(pd), fixed(ph)]
    sec_e, xh2_e, dg2_e, inv2_e = call(
        encoder_in, meta, (5,),
        [rows_chunk(tokens_t)] + halo + w_inner + [fixed(eye), fixed(pd), fixed(ph)],
        [out_fixed((rows, ext, LANES), BF), out_chunks(inner, BF), out_chunks(inner, BF), out_chunks(8, F32)],
        [scr((inner, width), BF), pds(2), phs(3), chunk_f, chunk_b, hid_f, hid_b],
        name="encoder_in", us=16,
    )
    parts2, sec_e = lax.optimization_barrier((parts2, sec_e))
    bundle2 = placed_parts(parts2)
    bundle2b = flip(bundle2, "pipe", 1)
    w_conv = [part(bundle2, 2 * PIECE, 0), part(bundle2b, 2 * PIECE, 0)]
    w_outer = [part(bundle2, PIECE, 2), part(bundle2b, PIECE, 2)]
    out_e, xh3_e, dg3_e, inv3_e, third_e, sec_d, xh2_d, dg2_d, inv2_d = call(
        encoder_out, meta, (5,),
        [fixed(sec_e), fixed(codes), fixed(code_cols), rows_chunk(tokens_t)] + halo + w_conv + w_outer + w_inner + last_ins,
        [
            out_chunks(width, F32), out_chunks(inner, BF), out_chunks(inner, BF), out_chunks(8, F32), out_chunks(TILE, BF),
            out_fixed((rows, inner, ext), BF), out_chunks(inner, BF), out_chunks(inner, BF), out_chunks(8, F32),
        ],
        [
            scr((inner, 5 * LANES), BF), scr((width, inner), BF), scr((inner, width), BF), pds(3), phs(6),
            scr((2 * CHUNK, 5 * LANES), BF), hid_f, hid_b, chunk_b, hid_b,
        ],
        name="encoder_out", us=32,
    )
    final = (jax.ShapeDtypeStruct((rows_all, width, length), F32), pl.BlockSpec((2, width, CHUNK), own_index))
    sent = (
        jax.ShapeDtypeStruct((rows, width, length), BF),
        pl.BlockSpec((2, width, CHUNK), lambda c, m: (0, 0, jnp.maximum(c - 1, 0))),
    )
    mine_out, other_out, mixed_d, go_d, gc_d = call(
        decoder_out, meta, (5,),
        [fixed(sec_d), fixed(codes), per_step(out_e), rows_chunk(cotangent_t)] + halo + w_conv + w_outer + last_ins,
        [
            final, sent, out_fixed((rows, inner, ext), BF), out_fixed((width, TILE)), out_fixed((3 * inner, TILE)),
        ],
        [
            scr((inner, 3 * inner), BF), scr((width, inner), BF), scr((inner, width), BF), pds(1), phs(3),
            scr((3 * inner, 2 * CHUNK), BF), hid_f, hid_b, chunk_f, both_b, hid_b, hid_b, hid_b, scr((2, 8, CHUNK), F32),
            pds(1), phs(3),
        ],
        name="decoder_out", us=30,
    )
    grad_d, mixed_e, gi_d, go_e = call(
        decoder_back, meta, (5,),
        [
            fixed(mixed_d), fixed(codes), per_step(xh2_d), per_step(dg2_d), per_step(inv2_d), per_step(out_e),
            rows_chunk(cotangent_t),
        ]
        + halo + [per_step(xh3_e), per_step(dg3_e), per_step(inv3_e), per_step(third_e)]
        + w_conv + w_inner + w_outer + last_ins,
        [out_chunks(width, F32), out_fixed((rows, ext, LANES), BF), out_fixed((width, TILE)), out_fixed((width, TILE))],
        [
            scr((inner, 3 * inner), BF), scr((width, inner), BF), scr((inner, width), BF), pds(2), phs(2),
            scr((3 * inner, 2 * CHUNK), BF), hid_f, hid_b, hid_b, both_b, both_b, chunk_f, pds(3), phs(6),
        ],
        name="decoder_back", us=40,
    )
    mine_grad, other_grad, gi_e, gc_e = call(
        encoder_back, meta, (4,),
        [
            fixed(mixed_e), fixed(sec_e), fixed(code_cols), per_step(xh2_e, 4), per_step(dg2_e, 4), per_step(inv2_e, 4),
            (tokens_t, pl.BlockSpec((2, width, CHUNK), lambda c, m: (m[0], 0, c))), per_step(grad_d, 4),
        ]
        + w_conv + w_inner + last_ins,
        [
            (final[0], pl.BlockSpec((2, width, CHUNK), lambda c, m: (m[0], 0, c))),
            (sent[0], pl.BlockSpec((2, width, CHUNK), lambda c, m: (0, 0, c))),
            out_fixed((width, TILE)), out_fixed((5 * inner, TILE)),
        ],
        [
            scr((inner, 5 * LANES), BF), scr((width, inner), BF), pds(2), phs(1),
            scr((2 * CHUNK, 5 * LANES), BF), scr((2 * CHUNK, 5 * LANES), BF), scr((TILE, 5 * LANES), F32), hid_f, hid_b, both_b, chunk_f, pds(2), phs(3),
        ],
        name="encoder_back", us=32,
    )

    def finish(mine, other):
        block = (1, width // 2, length)
        return jnp.transpose(
            call(
                fill_rows, meta, (2 * rows,),
                [
                    (flip(other, "pipe", 1), pl.BlockSpec(block, lambda c, m: (c // 2, c % 2, 0))),
                    (mine, pl.BlockSpec(memory_space=pl.ANY)),
                ],
                [(final[0], pl.BlockSpec(block, lambda c, m: (rows - rows * m[0] + c // 2, c % 2, 0)))],
                aliases={2: 0}, name="fill_rows", us=7,
            )[0],
            (0, 2, 1),
        )

    section_output = finish(mine_out, other_out)[None]

    taps_rows = 4 * inner
    kept, sent = call(
        pack_grads, meta, (1,), [fixed(x) for x in (gi_e, go_e, gc_e, gi_d, go_d, gc_d)],
        [out_fixed((2 * width + taps_rows, TILE)), out_fixed((2 * width + taps_rows, TILE), BF)],
        name="pack_grads", us=4,
    )
    kept = kept + flip(sent, "pipe", 1).astype(F32)
    parts, section_output = spread_over(kept, "seq", section_output)
    input_gradient = finish(mine_grad, other_grad)[None]
    summed, input_gradient = collect_over(parts, "seq", input_gradient)
    grads_inner, grads_outer = summed[:width], summed[width : 2 * width]
    conv_sum = summed[2 * width :]
    conv_other = flip(conv_sum, "pipe", 1)
    summed_f = [x.astype(F32) for x in (grads_inner, grads_outer)]
    conv_first = jnp.where(encoder_side, conv_sum, conv_other)
    conv_second = jnp.where(encoder_side, conv_other, conv_sum)
    grad_conv_e = jnp.concatenate([conv_first, conv_second[:inner]], axis=0)[:, :loc].astype(F32).reshape(5, inner, loc)
    grad_conv_d = conv_second[inner:, :loc].astype(F32).reshape(3, inner, loc)
    grad_inner = summed_f[0][:, :loc]
    grad_outer = jnp.transpose(summed_f[1][:, :loc])
    wide = [summed_f[0][:, FREE], summed_f[0][:, FREE + 1], summed_f[1][:, FREE]]
    narrow = jnp.concatenate([summed_f[0][:inner, FREE + 2 : FREE + 5], summed_f[1][:inner, FREE + 1 : FREE + 4]], axis=1)
    narrow = jnp.transpose(lax.dynamic_slice_in_dim(narrow, tensor * loc, loc, 0))

    return (
        section_output,
        input_gradient,
        wide[0][None],
        wide[1][None],
        grad_inner[None],
        narrow[2][None],
        narrow[0][None],
        narrow[1][None],
        grad_conv_e,
        grad_conv_d,
        narrow[5][None],
        narrow[3][None],
        narrow[4][None],
        grad_outer[None],
        wide[2][None],
    )


def solution(mesh):
    return jax.shard_map(
        on_device,
        mesh=mesh,
        in_specs=(
            P(None, "seq", None),
            P(None, "seq"),
            P(None, "seq"),
            P(None, "seq", None),
            P("pipe", None),
            P("pipe", None),
            P("pipe", None, "tensor"),
            P("pipe", "tensor"),
            P("pipe", "tensor"),
            P("pipe", "tensor"),
            P(None, None, "tensor"),
            P(None, None, "tensor"),
            P("pipe", "tensor"),
            P("pipe", "tensor"),
            P("pipe", "tensor"),
            P("pipe", "tensor", None),
            P("pipe", None),
        ),
        out_specs=(
            P("pipe", None, "seq", None),
            P("pipe", None, "seq", None),
            P("pipe", None),
            P("pipe", None),
            P("pipe", None, "tensor"),
            P("pipe", "tensor"),
            P("pipe", "tensor"),
            P("pipe", "tensor"),
            P(None, None, "tensor"),
            P(None, None, "tensor"),
            P("pipe", "tensor"),
            P("pipe", "tensor"),
            P("pipe", "tensor"),
            P("pipe", "tensor", None),
            P("pipe", None),
        ),
        check_vma=False,
    )
```

```python
import functools
import math

import jax
import jax.numpy as jnp
from jax import lax
from jax.experimental import pallas as pl
from jax.experimental.pallas import tpu as pltpu
from jax.sharding import PartitionSpec as P

SPACING = 16
EPSILON = 1e-05
BF = jnp.bfloat16
F32 = jnp.float32
LANES = 512
TILE = 128
CHUNK = 256
BLOCK = 16
PIECE = 208
ROOT = math.sqrt(2.0 / math.pi)
CUBIC = 0.044715
E_OFFSETS = tuple(SPACING * (k - 2) for k in range(5))
D_OFFSETS = (-2, -1, 0)
VMEM = 60 * 1024 * 1024
FREE = 120
COT_TURNS = (96, 48)


def dot(a, b):
    return lax.dot_general(a, b, (((1,), (0,)), ((), ())), preferred_element_type=F32)


def dot_nt(a, b):
    return lax.dot_general(a, b, (((1,), (1,)), ((), ())), preferred_element_type=F32)


def pair(column):
    return jnp.concatenate([column, column], axis=1)


def row_sum(values):
    return jnp.sum(values, axis=0, keepdims=True)


def moments(get, count):
    total = square = None
    for j in range(0, count, BLOCK):
        x = get(j)
        total = x if total is None else total + x
        square = x * x if square is None else square + x * x
    center = row_sum(total) * (1.0 / count)
    inverse = lax.rsqrt(row_sum(square) * (1.0 / count) - center * center + EPSILON)
    return center * inverse, inverse


def gate(half):
    square = half * half
    return jnp.tanh(half * (2 * ROOT + (8 * CUBIC * ROOT) * square)), square


def slope(half, tanh, square):
    return (1.0 + tanh) * (0.5 + (half - half * tanh) * (ROOT + (12 * CUBIC * ROOT) * square))


def spread(target, source, columns, *whole):
    for n, c in enumerate(columns):
        value = jnp.broadcast_to(source[:, c : c + 1], target.shape[1:])
        target[n] = value if n in [w - 1 for w in whole] else 0.5 * value


def param(ref, n, j):
    return pair(ref[n, j : j + BLOCK, :])


def placed(sel, a_ref, b_ref, lo):
    parts = []
    for q in range(a_ref.shape[0]):
        part = jnp.where(sel, a_ref[q, lo : lo + PIECE, :], b_ref[q, lo : lo + PIECE, :])
        parts.append(part.astype(F32)[:200])
    return jnp.concatenate(parts, axis=0).astype(BF)


def tap_of(sel, a_ref, b_ref, tap, inner):
    q = tap % 4
    first, second = a_ref[q, :inner, :], b_ref[q, :inner, :]
    return jnp.where(sel, first, second) if tap < 4 else jnp.where(sel, second, first)


def drive(live, *streams):
    def stage(fn):
        @pl.when(live)
        def _():
            fn()

    count = max(len(x) for x in streams)
    for slot in range(count + 1):
        here = [s[slot - n] for n, s in enumerate(streams) if 0 <= slot - n < len(s)]
        if slot % 2 == 0:
            here.reverse()
        stage(lambda here=here: [fn() for fn in here])


def tiles_of(step):
    return jnp.where(step == 0, 1, 2 * step), jnp.where(step == 0, 10, 2 * step + 1)


def at_tile(a, count=1):
    return pl.ds(pl.multiple_of(a * TILE, TILE), count * TILE)


def code_rows(code_ref, n, a, offsets):
    window = code_ref[n, :, at_tile(a - 1, 3)]
    here = window[:, TILE : 2 * TILE]
    return [(window[:, TILE + o : 2 * TILE + o] == here).astype(F32) for o in offsets], (here > 0.5).astype(F32)


def taps(cat_ref, ref, code_ref, n, step, offsets, count):
    kept = []
    for half, a in enumerate(tiles_of(step)):
        masks, keep = code_rows(code_ref, n, a, offsets)
        kept.append(keep)
        lanes = slice(n * CHUNK + half * TILE, n * CHUNK + (half + 1) * TILE)
        window = ref[n, :, at_tile(a - 1, 3)]
        for k, offset in enumerate(offsets):
            piece = window[:, TILE + offset : 2 * TILE + offset]
            if offset:
                piece = piece * masks[k].astype(BF)
            cat_ref[k * count : (k + 1) * count, lanes] = piece
    return jnp.concatenate(kept, axis=1)


def row_taps(cat_ref, ref, col_ref, n, step, offsets):
    for half, a in enumerate(tiles_of(step)):
        here = col_ref[n, at_tile(a), :]
        rows = slice(n * CHUNK + half * TILE, n * CHUNK + (half + 1) * TILE)
        for k, offset in enumerate(offsets):
            there = pl.ds(pl.multiple_of(a * TILE + offset, BLOCK), TILE)
            piece = ref[n, there, :]
            if offset:
                mask = (col_ref[n, there, :] == here).astype(BF)
                piece = piece * jnp.concatenate([mask] * (LANES // TILE), axis=1)
            cat_ref[rows, k * LANES : (k + 1) * LANES] = piece


def put_rows(ext_ref, n, step, values):
    turned = jnp.transpose(values[...])
    for half, a in enumerate(tiles_of(step)):
        ext_ref[n, at_tile(a), 0 : turned.shape[1]] = turned[half * TILE : (half + 1) * TILE, :]


def keep_row(code_ref, n, step):
    return jnp.concatenate([(code_ref[n, :, at_tile(a)] > 0.5).astype(F32) for a in tiles_of(step)], axis=1)


def put(ext_ref, n, step, values):
    for half, a in enumerate(tiles_of(step)):
        ext_ref[n, :, at_tile(a)] = values[:, half * TILE : (half + 1) * TILE]


def blank_ends(ext_ref):
    for a in (0, 11):
        ext_ref[:, :, a * TILE : (a + 1) * TILE] = jnp.zeros(ext_ref.shape[:2] + (TILE,), BF)


def from_sums(total, square, count):
    center = row_sum(total) * (1.0 / count)
    inverse = lax.rsqrt(row_sum(square) * (1.0 / count) - center * center + EPSILON)
    return center * inverse, inverse


def biased(hid_ref, ph, n):
    count = hid_ref.shape[0]
    total = square = None
    for j in range(0, count, BLOCK):
        x = hid_ref[j : j + BLOCK, :] + param(ph, n, j)
        hid_ref[j : j + BLOCK, :] = x
        total = x if total is None else total + x
        square = x * x if square is None else square + x * x
    return from_sums(total, square, count)


def activate(hid_ref, stats, ph, gain, bias, out_ref, xh_ref, dg_ref, inv_ref):
    shift, inverse = stats
    inv_ref[...] = jnp.broadcast_to(inverse, inv_ref.shape)
    for j in range(0, hid_ref.shape[0], BLOCK):
        scaled = hid_ref[j : j + BLOCK, :] * inverse - shift
        half = scaled * param(ph, gain, j) + param(ph, bias, j)
        tanh, square = gate(half)
        out_ref[j : j + BLOCK, :] = (half + half * tanh).astype(BF)
        xh_ref[j : j + BLOCK, :] = scaled.astype(BF)
        dg_ref[j : j + BLOCK, :] = slope(half, tanh, square).astype(BF)


def first_of(x_ref, stats, pd, gain, out_ref, slope_ref=None, scaled_ref=None):
    shift, inverse = stats
    for j in range(0, x_ref.shape[0], BLOCK):
        scaled = x_ref[j : j + BLOCK, :] * inverse - shift
        half = scaled * param(pd, gain, j) + param(pd, gain + 1, j)
        tanh, square = gate(half)
        out_ref[j : j + BLOCK, :] = (half + half * tanh).astype(BF)
        if slope_ref is not None:
            slope_ref[j : j + BLOCK, :] = slope(half, tanh, square)
            scaled_ref[j : j + BLOCK, :] = scaled


def moments_of(x_ref):
    return moments(lambda j: x_ref[j : j + BLOCK, :], x_ref.shape[0])


def halves(values):
    return values[:, :TILE] + values[:, TILE:]


def norm_back(grad_ref, xh_ref, dg_ref, inverse, ph, gain, low_ref, acc, base):
    count = low_ref.shape[0]
    first = second = None
    for j in range(0, count, BLOCK):
        down = grad_ref[j : j + BLOCK, :] * dg_ref[j : j + BLOCK, :].astype(F32)
        cross = down * xh_ref[j : j + BLOCK, :].astype(F32)
        acc[base, j : j + BLOCK, :] += halves(cross)
        acc[base + 1, j : j + BLOCK, :] += halves(down)
        g = param(ph, gain, j)
        weighted = down * g
        grad_ref[j : j + BLOCK, :] = weighted
        first = weighted if first is None else first + weighted
        second = cross * g if second is None else second + cross * g
    twice = inverse * 2.0
    first = row_sum(first) * (twice * (1.0 / count))
    second = row_sum(second) * (twice * (1.0 / count))
    for j in range(0, count, BLOCK):
        result = grad_ref[j : j + BLOCK, :] * twice - first - xh_ref[j : j + BLOCK, :].astype(F32) * second
        low_ref[j : j + BLOCK, :] = result.astype(BF)
        acc[base + 2, j : j + BLOCK, :] += halves(result)


def own_rows(pick_ref, values):
    return dot(pick_ref[...], values).astype(BF)


def columns(target, lane, acc, order):
    count = acc.shape[1]
    for n, k in enumerate(order):
        target[0:count, lane + n : lane + n + 1] = jnp.sum(acc[k], axis=1, keepdims=True)


def clear(step, *refs):
    @pl.when(step <= 1)
    def _():
        for ref in refs:
            ref[...] = jnp.zeros_like(ref)


def turned(tile, by):
    return pltpu.roll(tile, by, 1) if by else tile


def fetch(step, target, own_ref, before_ref, after_ref, turns):
    @pl.when(step == 0)
    def _():
        width = target.shape[1]
        for n in range(2):
            target[n, :, 0:TILE] = turned(before_ref[n, 0:width, :].astype(F32), turns[0])
            target[n, :, TILE:] = turned(after_ref[n, 0:width, :].astype(F32), turns[1])

    @pl.when(step > 0)
    def _():
        target[...] = own_ref[...]


def encoder_in(meta, tok_ref, before_ref, after_ref, a_ref, b_ref, eye_ref, pd_ref, ph_ref,
               sec_ref, xh_ref, dg_ref, inv_ref, wi, pd, ph, x_s, first_s, hid_s, sec_s):
    step = pl.program_id(0)

    @pl.when(step == 0)
    def _():
        spread(pd, pd_ref, (0, 1))
        spread(ph, ph_ref, (0, 1, 2), 1)
        wi[...] = dot_nt(eye_ref[...], placed(meta[0] == 0, a_ref, b_ref, 0)).astype(BF)
        sec_ref[...] = jnp.zeros_like(sec_ref)

    fetch(step, x_s, tok_ref, before_ref, after_ref, (0, 0))

    def stream(n):
        def enter():
            first_of(x_s.at[n], moments_of(x_s.at[n]), pd, 0, first_s.at[n])

        def product():
            hid_s[n] = dot(wi[...], first_s[n])

        def leave():
            stats = biased(hid_s.at[n], ph, 0)
            activate(hid_s.at[n], stats, ph, 1, 2, sec_s.at[n], xh_ref.at[n], dg_ref.at[n], inv_ref.at[n])
            put_rows(sec_ref, n, step, sec_s.at[n])

        return [enter, product, leave]

    drive(meta[0] >= 0, stream(0), stream(1))


def encoder_out(meta, sec_ref, code_ref, col_ref, tok_ref, before_ref, after_ref, a_ref, b_ref, ao_ref, bo_ref, ai_ref, bi_ref,
                eye_ref, pick_ref, pd_ref, ph_ref,
                out_ref, xh3_ref, dg3_ref, inv3_ref, third_ref, secd_ref, xh2_ref, dg2_ref, inv2_ref,
                wc, wo, wi, pd, ph, cat, hid_s, third_s, first_s, sec_s, wide_s):
    step = pl.program_id(0)
    width = tok_ref.shape[1]
    inner = eye_ref.shape[0]

    @pl.when(step == 0)
    def _():
        spread(pd, pd_ref, (2, 3, 4), 1)
        spread(ph, ph_ref, (3, 4, 5, 6, 7, 8), 1, 4)
        sel = meta[0] == 0
        wc[...] = jnp.zeros_like(wc)
        for k in range(5):
            wc[:, k * LANES : k * LANES + inner] = dot_nt(eye_ref[...], tap_of(sel, a_ref, b_ref, k, inner)).astype(BF)
        wo[...] = dot_nt(placed(sel, ao_ref, bo_ref, 0), eye_ref[...]).astype(BF)
        wi[...] = dot_nt(eye_ref[...], placed(sel, bi_ref, ai_ref, 0)).astype(BF)
        blank_ends(secd_ref)

    fetch(step, out_ref, tok_ref, before_ref, after_ref, (0, 0))

    def stream(n):
        rows = slice(n * CHUNK, (n + 1) * CHUNK)

        def sources():
            row_taps(cat, sec_ref, col_ref, n, step, E_OFFSETS)

        def convolve():
            hid_s[n] = dot_nt(wc[...], cat[rows, :])

        def activate3():
            stats = biased(hid_s.at[n], ph, 0)
            activate(hid_s.at[n], stats, ph, 1, 2, third_s.at[n], xh3_ref.at[n], dg3_ref.at[n], inv3_ref.at[n])

        def project():
            wide_s[n] = dot(wo[...], third_s[n])
            third_ref[n] = own_rows(pick_ref, third_s[n])

        def add():
            kept = jnp.broadcast_to(keep_row(code_ref, n, step), (BLOCK, CHUNK))
            total = square = None
            for j in range(0, width, BLOCK):
                x = out_ref[n, j : j + BLOCK, :] + kept * (wide_s[n, j : j + BLOCK, :] + param(pd, 0, j))
                out_ref[n, j : j + BLOCK, :] = x
                total = x if total is None else total + x
                square = x * x if square is None else square + x * x
            first_of(out_ref.at[n], from_sums(total, square, width), pd, 1, first_s.at[n])

        def product():
            hid_s[n] = dot(wi[...], first_s[n])

        def leave():
            stats = biased(hid_s.at[n], ph, 3)
            activate(hid_s.at[n], stats, ph, 4, 5, sec_s.at[n], xh2_ref.at[n], dg2_ref.at[n], inv2_ref.at[n])
            put(secd_ref, n, step, sec_s.at[n])

        return [sources, convolve, activate3, project, add, product, leave]

    drive(meta[0] >= 0, stream(0), stream(1))


def decoder_out(meta, sec_ref, code_ref, in_ref, cot_ref, before_ref, after_ref, a_ref, b_ref, ao_ref, bo_ref, eye_ref, pick_ref,
                pd_ref, ph_ref,
                mine_ref, other_ref, mixed_ref, go_ref, gc_ref,
                wc, wo, wob, pd, ph, cat, hid_s, third_s, cot_f, cot_s, low_s, xh_s, dg_s, inv_s, grad_s, accd, acch):
    step = pl.program_id(0)
    width = in_ref.shape[1]
    inner = eye_ref.shape[0]

    @pl.when(step == 0)
    def _():
        spread(pd, pd_ref, (5,), 1)
        spread(ph, ph_ref, (9, 10, 11), 1)
        sel = meta[0] == 0
        for k in range(3):
            wc[:, k * inner : (k + 1) * inner] = dot_nt(eye_ref[...], tap_of(sel, a_ref, b_ref, 5 + k, inner)).astype(BF)
        outer = placed(sel, bo_ref, ao_ref, 0)
        wo[...] = dot_nt(outer, eye_ref[...]).astype(BF)
        wob[...] = dot_nt(eye_ref[...], outer).astype(BF)
        blank_ends(mixed_ref)

    clear(step, go_ref, gc_ref, accd, acch)
    fetch(step, cot_f, cot_ref, before_ref, after_ref, COT_TURNS)
    encoder_side = meta[0] == 0

    def stream(n):
        lanes = slice(n * CHUNK, (n + 1) * CHUNK)

        def sources():
            kept = jnp.broadcast_to(keep_row(code_ref, n, step), (BLOCK, CHUNK))
            for j in range(0, width, BLOCK):
                branch = kept * cot_f[n, j : j + BLOCK, :]
                accd[0, j : j + BLOCK, :] += halves(branch)
                cot_s[j : j + BLOCK, lanes] = branch.astype(BF)
            taps(cat, sec_ref, code_ref, n, step, D_OFFSETS, inner)

        def convolve():
            hid_s[n] = dot(wc[...], cat[:, lanes])
            grad_s[n] = dot(wob[...], cot_s[:, lanes])

        def middle():
            stats = biased(hid_s.at[n], ph, 0)
            activate(hid_s.at[n], stats, ph, 1, 2, third_s.at[n], xh_s.at[n], dg_s.at[n], inv_s.at[n])
            norm_back(grad_s.at[n], xh_s.at[n], dg_s.at[n], stats[1], ph, 1, low_s.at[n], acch, 0)
            put(mixed_ref, n, step, low_s.at[n])

        def project():
            cot_f[n] = dot(wo[...], third_s[n])

        def add():
            kept = jnp.broadcast_to(keep_row(code_ref, n, step), (BLOCK, CHUNK))
            for j in range(0, width, BLOCK):
                x = in_ref[n, j : j + BLOCK, :]
                y = x + kept * (cot_f[n, j : j + BLOCK, :] + param(pd, 0, j))
                mine_ref[n, j : j + BLOCK, :] = jnp.where(encoder_side, x, y)
                other_ref[n, j : j + BLOCK, :] = jnp.where(encoder_side, y, x).astype(BF)

        return [sources, convolve, middle, project, add]

    def weights():
        picked = own_rows(pick_ref, jnp.concatenate([third_s[0], third_s[1], low_s[0], low_s[1]], axis=1))
        go_ref[...] += dot_nt(cot_s[...], picked[:, : 2 * CHUNK])
        gc_ref[...] += dot_nt(cat[...], picked[:, 2 * CHUNK :])

    drive(meta[0] >= 0, stream(0) + [weights], stream(1))

    @pl.when(step == 4)
    def _():
        columns(go_ref, FREE, accd, (0,))
        columns(go_ref, FREE + 1, acch, (0, 1, 2))


def input_back(wide_ref, scaled_ref, inverse, dg1_ref, pd, accd, finish):
    width = wide_ref.shape[0]
    first = second = None
    for j in range(0, width, BLOCK):
        scaled = scaled_ref[j : j + BLOCK, :]
        down = wide_ref[j : j + BLOCK, :] * dg1_ref[j : j + BLOCK, :]
        cross = down * scaled
        accd[0, j : j + BLOCK, :] += halves(cross)
        accd[1, j : j + BLOCK, :] += halves(down)
        g = param(pd, 0, j)
        weighted = down * g
        wide_ref[j : j + BLOCK, :] = weighted
        first = weighted if first is None else first + weighted
        second = cross * g if second is None else second + cross * g
    twice = inverse * 2.0
    first = row_sum(first) * (twice * (1.0 / width))
    second = row_sum(second) * (twice * (1.0 / width))
    for j in range(0, width, BLOCK):
        finish(j, wide_ref[j : j + BLOCK, :] * twice - first - scaled_ref[j : j + BLOCK, :] * second)


def decoder_back(meta, mixed_ref, code_ref, xh2_ref, dg2_ref, inv2_ref, in_ref, cot_ref, before_ref, after_ref,
                 xh3_ref, dg3_ref, inv3_ref, third_ref, a_ref, b_ref, ai_ref, bi_ref, ao_ref, bo_ref, eye_ref, pick_ref,
                 pd_ref, ph_ref,
                 grad_ref, low3_ref, gi_ref, go_ref,
                 wc, wib, wob, pd, ph, cat, hid_s, low_s, low3_s, first_s, branch_s, dg1_s, wide_s, scaled_s, inv1_s, accd, acch):
    step = pl.program_id(0)
    inner = eye_ref.shape[0]

    @pl.when(step == 0)
    def _():
        spread(pd, pd_ref, (3, 4))
        spread(ph, ph_ref, (7, 4))
        sel = meta[0] == 0
        for k in range(3):
            wc[:, k * inner : (k + 1) * inner] = dot_nt(tap_of(sel, a_ref, b_ref, 5 + k, inner), eye_ref[...]).astype(BF)
        wib[...] = dot_nt(placed(sel, bi_ref, ai_ref, 0), eye_ref[...]).astype(BF)
        wob[...] = dot_nt(eye_ref[...], placed(sel, ao_ref, bo_ref, 0)).astype(BF)
        low3_ref[...] = jnp.zeros_like(low3_ref)

    clear(step, gi_ref, go_ref, accd, acch)
    fetch(step, grad_ref, cot_ref, before_ref, after_ref, COT_TURNS)

    def stream(n):
        lanes = slice(n * CHUNK, (n + 1) * CHUNK)

        def sources():
            taps(cat, mixed_ref, code_ref, n, step, tuple(-o for o in D_OFFSETS), inner)
            stats = moments_of(in_ref.at[n])
            inv1_s[n] = jnp.broadcast_to(stats[1], inv1_s.shape[1:])
            first_of(in_ref.at[n], stats, pd, 0, first_s.at[:, lanes], dg1_s.at[n], scaled_s.at[n])

        def convolve():
            hid_s[n] = dot(wc[...], cat[:, lanes])

        def second():
            norm_back(hid_s.at[n], xh2_ref.at[n], dg2_ref.at[n], inv2_ref[n, 0:1, :], ph, 0, low_s.at[n], acch, 0)

        def project():
            wide_s[n] = dot(wib[...], low_s[n])

        def leave():
            kept = jnp.broadcast_to(keep_row(code_ref, n, step), (BLOCK, CHUNK))

            def finish(j, value):
                value = grad_ref[n, j : j + BLOCK, :] + value
                grad_ref[n, j : j + BLOCK, :] = value
                branch = kept * value
                accd[2, j : j + BLOCK, :] += halves(branch)
                branch_s[j : j + BLOCK, lanes] = branch.astype(BF)

            input_back(wide_s.at[n], scaled_s.at[n], inv1_s[n, 0:1, :], dg1_s.at[n], pd, accd, finish)

        def outward():
            hid_s[n] = dot(wob[...], branch_s[:, lanes])

        def third():
            norm_back(hid_s.at[n], xh3_ref.at[n], dg3_ref.at[n], inv3_ref[n, 0:1, :], ph, 1, low3_s.at[n], acch, 3)
            put_rows(low3_ref, n, step, low3_s.at[n])

        return [sources, convolve, second, project, leave, outward, third]

    def weights():
        low = own_rows(pick_ref, jnp.concatenate([low_s[0], low_s[1]], axis=1))
        third = jnp.concatenate([third_ref[n] for n in range(2)], axis=1)
        gi_ref[...] += dot_nt(first_s[...], low)
        go_ref[...] += dot_nt(branch_s[...], third)

    drive(meta[0] >= 0, stream(0) + [weights], stream(1))

    @pl.when(step == 4)
    def _():
        columns(gi_ref, FREE, accd, (0, 1))
        columns(gi_ref, FREE + 2, acch, (0, 1, 2))
        columns(go_ref, FREE, accd, (2,))
        columns(go_ref, FREE + 1, acch, (3, 4, 5))


def encoder_back(meta, mixed_ref, sec_ref, col_ref, xh2_ref, dg2_ref, inv2_ref, in_ref, later_ref, a_ref, b_ref,
                 ai_ref, bi_ref, eye_ref, pick_ref, pd_ref, ph_ref, recv_ref, final_ref,
                 mine_ref, other_ref, gi_ref, gc_ref, out_ref,
                 wc, wib, pd, ph, cat, catw, gc_s, hid_s, low_s, first_s, dg1_s, wide_s, scaled_s, inv1_s, accd, acch):
    del final_ref
    step = pl.program_id(0) + 1
    inner = eye_ref.shape[0]

    @pl.when(step == 1)
    def _():
        spread(pd, pd_ref, (0, 1))
        spread(ph, ph_ref, (1,))
        sel = meta[0] == 0
        wc[...] = jnp.zeros_like(wc)
        for k in range(5):
            wc[:, k * LANES : k * LANES + inner] = dot_nt(tap_of(sel, a_ref, b_ref, k, inner), eye_ref[...]).astype(BF)
        wib[...] = dot_nt(placed(sel, ai_ref, bi_ref, 0), eye_ref[...]).astype(BF)

    clear(step, gi_ref, gc_s, accd, acch)
    encoder_side = meta[0] == 0

    def stream(n):
        lanes = slice(n * CHUNK, (n + 1) * CHUNK)

        def sources():
            out_ref[n] = recv_ref[n].astype(F32)
            row_taps(cat, mixed_ref, col_ref, n, step, tuple(-o for o in E_OFFSETS))
            row_taps(catw, sec_ref, col_ref, n, step, E_OFFSETS)
            stats = moments_of(in_ref.at[n])
            inv1_s[n] = jnp.broadcast_to(stats[1], inv1_s.shape[1:])
            first_of(in_ref.at[n], stats, pd, 0, first_s.at[:, lanes], dg1_s.at[n], scaled_s.at[n])

        def convolve():
            hid_s[n] = dot_nt(wc[...], cat[lanes, :])

        def second():
            norm_back(hid_s.at[n], xh2_ref.at[n], dg2_ref.at[n], inv2_ref[n, 0:1, :], ph, 0, low_s.at[n], acch, 0)

        def project():
            wide_s[n] = dot(wib[...], low_s[n])
            if n:
                mixed = [
                    dot_nt(pick_ref[...], mixed_ref[r, at_tile(2 * step, 2), 0:inner]).astype(BF) for r in range(2)
                ]
                gc_s[...] += dot(jnp.concatenate(mixed, axis=1), catw[...])

        def leave():
            def finish(j, value):
                later = later_ref[n, j : j + BLOCK, :]
                value = later + value
                mine_ref[n, j : j + BLOCK, :] = jnp.where(encoder_side, value, later)
                other_ref[n, j : j + BLOCK, :] = jnp.where(encoder_side, later, value).astype(BF)

            input_back(wide_s.at[n], scaled_s.at[n], inv1_s[n, 0:1, :], dg1_s.at[n], pd, accd, finish)

        return [sources, convolve, second, project, leave]

    def weights():
        low = own_rows(pick_ref, jnp.concatenate([low_s[0], low_s[1]], axis=1))
        gi_ref[...] += dot_nt(first_s[...], low)

    drive(meta[0] >= 0, stream(0) + [weights], stream(1))

    @pl.when(step == 4)
    def _():
        columns(gi_ref, FREE, accd, (0, 1))
        columns(gi_ref, FREE + 2, acch, (0, 1, 2))
        for k in range(5):
            gc_ref[k * inner : (k + 1) * inner, :] = jnp.transpose(gc_s[:, k * LANES : k * LANES + inner])


def fill_rows(meta, recv_ref, final_ref, out_ref):
    del meta, final_ref
    out_ref[...] = recv_ref[...].astype(F32)


def pack_edges(meta, tok_last, cot_last, tok_first, cot_first, code_last, code_first, tail_ref, head_ref):
    del meta
    width = tok_last.shape[1]
    lane = lax.broadcasted_iota(jnp.int32, (width, TILE), 1)
    for n in range(2):
        tail_ref[n, 0:width, :] = jnp.where(lane < 32, turned(cot_last[n], 32), tok_last[n]).astype(BF)
        head_ref[n, 0:width, :] = jnp.where(lane < 80, tok_first[n], turned(cot_first[n], 80)).astype(BF)
        tail_ref[n, width:, :] = jnp.broadcast_to(code_last[n], (BLOCK, TILE)).astype(BF)
        head_ref[n, width:, :] = jnp.broadcast_to(code_first[n], (BLOCK, TILE)).astype(BF)


def place_weights(place, own_ref, *refs):
    out_ref = refs[-1]
    for q in range(4):
        out_ref[q, :, at_tile(place[1])] = own_ref[q]
    for by in range(4):
        for slot in range(1, 4):
            out_ref[place[0] ^ by, :, at_tile(place[1] ^ slot)] = refs[by][slot - 1]


def pack_grads(meta, gie, goe, gce, gid, god, gcd, kept_ref, sent_ref):
    encoder_side = meta[0] == 0
    width, most = gie.shape[0], 4 * (gce.shape[0] // 5)
    pieces = [(gie[...], gid[...]), (goe[...], god[...])]
    pieces.append((gce[0:most, :], jnp.concatenate([gce[most:, :], gcd[...]], axis=0)))
    start = 0
    for e, d in pieces:
        rows = slice(start, start + e.shape[0])
        start += e.shape[0]
        kept_ref[rows, :] = jnp.where(encoder_side, e, d)
        sent_ref[rows, :] = jnp.where(encoder_side, d, e).astype(BF)


def call(body, meta, grid, ins, outs, scratch=(), aliases=None, name=None, us=3):
    return pl.pallas_call(
        body,
        grid_spec=pltpu.PrefetchScalarGridSpec(
            num_scalar_prefetch=1,
            grid=grid,
            in_specs=[s for _, s in ins],
            out_specs=[s for _, s in outs],
            scratch_shapes=list(scratch),
        ),
        out_shape=[s for s, _ in outs],
        input_output_aliases=aliases or {},
        compiler_params=pltpu.CompilerParams(
            dimension_semantics=("arbitrary",) * len(grid), vmem_limit_bytes=VMEM
        ),
        cost_estimate=pl.CostEstimate(flops=int(us * 1.0e9), bytes_accessed=int(us * 3.5e6), transcendentals=0),
        name=name,
    )(meta, *[a for a, _ in ins])


def per_step(array, steps=5):
    first = array.shape[0] // 2 - steps
    return (array, pl.BlockSpec((2,) + array.shape[1:], lambda c, m: (c + first, 0, 0)))


def own_index(c, m):
    return (m[0], 0, jnp.maximum(c - 1, 0))


def rows_chunk(array):
    return (array, pl.BlockSpec((2, array.shape[1], CHUNK), own_index))


def fixed(array):
    zeros = (0,) * array.ndim
    return (array, pl.BlockSpec(array.shape, lambda c, m: zeros))


def part(array, rows, index):
    return (array, pl.BlockSpec((array.shape[0], rows, array.shape[2]), lambda c, m: (0, index, 0)))


def out_chunks(rows, dtype):
    return (jax.ShapeDtypeStruct((10, rows, CHUNK), dtype), pl.BlockSpec((2, rows, CHUNK), lambda c, m: (c, 0, 0)))


def out_fixed(shape, dtype=F32):
    zeros = (0,) * len(shape)
    return (jax.ShapeDtypeStruct(shape, dtype), pl.BlockSpec(shape, lambda c, m: zeros))


def flip(x, axis, by):
    count = lax.axis_size(axis)
    return lax.ppermute(x, axis, [(i, i ^ by) for i in range(count)])


def gather(x, axis):
    me = lax.axis_index(axis)
    count = lax.axis_size(axis)
    result = jnp.zeros((count,) + x.shape, x.dtype)
    result = lax.dynamic_update_index_in_dim(result, x, me, 0)
    for by in range(1, count):
        result = lax.dynamic_update_index_in_dim(result, flip(x, axis, by), me ^ by, 0)
    return result


def gather_lanes(x, axis):
    me = lax.axis_index(axis)
    count = lax.axis_size(axis)
    lanes = x.shape[-1]
    result = jnp.zeros(x.shape[:-1] + (count * lanes,), x.dtype)
    result = lax.dynamic_update_slice_in_dim(result, x, me * lanes, 1)
    for by in range(1, count):
        result = lax.dynamic_update_slice_in_dim(result, flip(x, axis, by), (me ^ by) * lanes, 1)
    return result


def spread_over(x, axis, beside):
    count = lax.axis_size(axis)
    me = lax.axis_index(axis)
    parts = x.reshape((count, x.shape[0] // count) + x.shape[1:])
    low = parts.astype(BF)
    arrived = [
        flip(lax.dynamic_index_in_dim(low, me ^ by, 0, keepdims=False), axis, by) for by in range(1, count)
    ]
    arrived, beside = lax.optimization_barrier((arrived, beside))
    total = lax.dynamic_index_in_dim(parts, me, 0, keepdims=False)
    for part_of in arrived:
        total = total + part_of.astype(F32)
    return total.astype(BF), beside


def collect_over(x, axis):
    me = lax.axis_index(axis)
    count = lax.axis_size(axis)
    arrived = [flip(x, axis, by) for by in range(1, count)]
    result = jnp.zeros((count,) + x.shape, x.dtype)
    result = lax.dynamic_update_index_in_dim(result, x, me, 0)
    for by in range(1, count):
        result = lax.dynamic_update_index_in_dim(result, arrived[by - 1], me ^ by, 0)
    return result.reshape((count * x.shape[0],) + x.shape[1:])


def pad_to(x, axis, size):
    widths = [(0, 0)] * x.ndim
    widths[axis] = (0, size - x.shape[axis])
    return jnp.pad(x, widths)


def on_device(
    tokens, segments, pad_mask, cotangent, gain_first, bias_first, weight_inner, bias_inner, gain_middle, bias_middle,
    weight_conv_encoder, weight_conv_decoder, bias_conv, gain_last, bias_last, weight_outer, bias_outer,
):
    pipe, seq, tensor = (lax.axis_index(a) for a in ("pipe", "seq", "tensor"))
    n_pipe, n_seq, n_tensor = (lax.axis_size(a) for a in ("pipe", "seq", "tensor"))
    rows_all, length, width = tokens.shape
    rows = rows_all // n_pipe
    loc = weight_conv_encoder.shape[2]
    inner = weight_conv_encoder.shape[1]
    lanes = LANES // n_tensor
    encoder_side = pipe == 0
    meta = jnp.stack([pipe, tensor * loc]).astype(jnp.int32)
    tokens_t, cotangent_t = jnp.transpose(tokens, (0, 2, 1)), jnp.transpose(cotangent, (0, 2, 1))

    def mine_rows(array):
        return lax.dynamic_slice_in_dim(array, pipe * rows, rows, 0)

    codes = (mine_rows(jnp.where(pad_mask == 1, segments + 1, 0)).astype(F32) + 1.0)[:, None, :]
    last = length // TILE - 1

    def edge_tile(array, row, index):
        return (array, pl.BlockSpec((2, array.shape[1], TILE), lambda c, m: (m[0] if row else 0, 0, index)))

    edge_out = out_fixed((rows, width + BLOCK, TILE), BF)
    tail, head = call(
        pack_edges, meta, (1,),
        [
            edge_tile(tokens_t, True, last), edge_tile(cotangent_t, True, last),
            edge_tile(tokens_t, True, 0), edge_tile(cotangent_t, True, 0),
            edge_tile(codes, False, last), edge_tile(codes, False, 0),
        ],
        [edge_out, edge_out], name="pack_edges", us=4,
    )

    small = jnp.stack([bias_inner[0], gain_middle[0], bias_middle[0], bias_conv[0], gain_last[0], bias_last[0]])
    high = lax.reduce_precision(small, 8, 7)
    small = pad_to(jnp.concatenate([high, small - high], axis=0), 0, BLOCK)
    inner_all = pad_to(weight_inner[0].reshape(n_seq, width // n_seq, loc), 1, PIECE)
    inner_all = jnp.concatenate([inner_all, jnp.broadcast_to(small[None], (n_seq,) + small.shape)], axis=1)
    outer_all = pad_to(jnp.transpose(weight_outer[0]).reshape(n_seq, width // n_seq, loc), 1, PIECE)
    conv_all = pad_to(
        jnp.where(
            encoder_side,
            weight_conv_encoder[:4],
            jnp.concatenate([weight_conv_encoder[4:], weight_conv_decoder], axis=0),
        ), 1, 2 * PIECE,
    )

    def gathered(pieces, ahead=None, between=None):
        pieces = pad_to(pieces.astype(BF), 2, lanes)
        sent = lax.dynamic_index_in_dim(pieces, seq, 0, keepdims=False)
        if ahead is not None:
            sent, _ = lax.optimization_barrier((sent, ahead))
        if lanes != TILE or n_seq != 4:
            return gather(gather_lanes(sent, "tensor"), "seq")
        near = jnp.stack([flip(sent, "tensor", by) for by in range(1, 4)])
        if between is not None:
            near, _ = lax.optimization_barrier((near, between))
        return [pieces, near] + [flip(near, "seq", by) for by in range(1, 4)]

    def placed_parts(parts):
        if not isinstance(parts, list):
            return parts
        rows_in = parts[0].shape[1]
        return call(
            place_weights, jnp.stack([seq, tensor]).astype(jnp.int32), (1,), [fixed(x) for x in parts],
            [out_fixed((4, rows_in, LANES), BF)], name="place_weights", us=4,
        )[0]

    before = lax.ppermute(tail, "seq", [(i, i + 1) for i in range(n_seq - 1)])
    after = lax.ppermute(head, "seq", [(i + 1, i) for i in range(n_seq - 1)])
    parts1 = gathered(inner_all, None, (before, after))
    parts2 = gathered(jnp.concatenate([conv_all, outer_all], axis=1), (tail, head))
    bundle1 = placed_parts(parts1)
    large = jnp.stack([gain_first[0], bias_first[0], bias_outer[0]], axis=0)
    bundle1b, large2 = flip(bundle1, "pipe", 1), flip(large, "pipe", 1)
    def columns_of(mine, other):
        first, second = jnp.where(encoder_side, mine, other), jnp.where(encoder_side, other, mine)
        return pad_to(jnp.transpose(jnp.concatenate([first, second], axis=0)), 1, TILE)

    def small_of(bundle):
        values = bundle[0, PIECE : PIECE + 12].astype(F32)
        values = (values[:6] + values[6:]).reshape(6, n_tensor, lanes)
        return values[:, :, :loc].reshape(6, inner)

    ph, pd = columns_of(small_of(bundle1), small_of(bundle1b)), columns_of(large, large2)
    first_lane = jnp.arange(inner)
    first_lane = first_lane // loc * lanes + first_lane % loc
    eye = (first_lane[:, None] == jnp.arange(LANES)[None, :]).astype(BF)
    own = (jnp.arange(TILE)[:, None] + tensor * loc == jnp.arange(inner)[None, :]) & (jnp.arange(TILE)[:, None] < loc)
    own = own.astype(BF)
    w_inner = [part(bundle1, PIECE + BLOCK, 0), part(bundle1b, PIECE + BLOCK, 0)]
    none = jnp.zeros((rows, 1, TILE), F32)
    codes = jnp.concatenate(
        [none, before[:, width : width + 1].astype(F32), codes, after[:, width : width + 1].astype(F32), none], axis=2
    ) - 1.0
    code_cols = jnp.broadcast_to(codes[:, 0, :, None], (rows, codes.shape[2], TILE)).astype(BF)
    halo = [fixed(before), fixed(after)]

    ext = length + 4 * TILE
    scr = pltpu.VMEM
    chunk_f = scr((2, width, CHUNK), F32)
    chunk_b = scr((2, width, CHUNK), BF)
    both_b = scr((width, 2 * CHUNK), BF)
    hid_f = scr((2, inner, CHUNK), F32)
    hid_b = scr((2, inner, CHUNK), BF)

    def pds(n):
        return scr((n, width, TILE), F32)

    def phs(n):
        return scr((n, inner, TILE), F32)

    last_ins = [fixed(eye), fixed(own), fixed(pd), fixed(ph)]
    sec_e, xh2_e, dg2_e, inv2_e = call(
        encoder_in, meta, (5,),
        [rows_chunk(tokens_t)] + halo + w_inner + [fixed(eye), fixed(pd), fixed(ph)],
        [out_fixed((rows, ext, LANES), BF), out_chunks(inner, BF), out_chunks(inner, BF), out_chunks(8, F32)],
        [scr((inner, width), BF), pds(2), phs(3), chunk_f, chunk_b, hid_f, hid_b],
        name="encoder_in", us=16,
    )
    parts2, sec_e = lax.optimization_barrier((parts2, sec_e))
    bundle2 = placed_parts(parts2)
    bundle2b = flip(bundle2, "pipe", 1)
    w_conv = [part(bundle2, 2 * PIECE, 0), part(bundle2b, 2 * PIECE, 0)]
    w_outer = [part(bundle2, PIECE, 2), part(bundle2b, PIECE, 2)]
    out_e, xh3_e, dg3_e, inv3_e, third_e, sec_d, xh2_d, dg2_d, inv2_d = call(
        encoder_out, meta, (5,),
        [fixed(sec_e), fixed(codes), fixed(code_cols), rows_chunk(tokens_t)] + halo + w_conv + w_outer + w_inner + last_ins,
        [
            out_chunks(width, F32), out_chunks(inner, BF), out_chunks(inner, BF), out_chunks(8, F32), out_chunks(TILE, BF),
            out_fixed((rows, inner, ext), BF), out_chunks(inner, BF), out_chunks(inner, BF), out_chunks(8, F32),
        ],
        [
            scr((inner, 5 * LANES), BF), scr((width, inner), BF), scr((inner, width), BF), pds(3), phs(6),
            scr((2 * CHUNK, 5 * LANES), BF), hid_f, hid_b, chunk_b, hid_b, chunk_f,
        ],
        name="encoder_out", us=32,
    )
    final = (jax.ShapeDtypeStruct((rows_all, width, length), F32), pl.BlockSpec((2, width, CHUNK), own_index))
    sent = (
        jax.ShapeDtypeStruct((rows, width, length), BF),
        pl.BlockSpec((2, width, CHUNK), lambda c, m: (0, 0, jnp.maximum(c - 1, 0))),
    )
    mine_out, other_out, mixed_d, go_d, gc_d = call(
        decoder_out, meta, (5,),
        [fixed(sec_d), fixed(codes), per_step(out_e), rows_chunk(cotangent_t)] + halo + w_conv + w_outer + last_ins,
        [
            final, sent, out_fixed((rows, inner, ext), BF), out_fixed((width, TILE)), out_fixed((3 * inner, TILE)),
        ],
        [
            scr((inner, 3 * inner), BF), scr((width, inner), BF), scr((inner, width), BF), pds(1), phs(3),
            scr((3 * inner, 2 * CHUNK), BF), hid_f, hid_b, chunk_f, both_b, hid_b, hid_b, hid_b, scr((2, 8, CHUNK), F32), hid_f,
            pds(1), phs(3),
        ],
        name="decoder_out", us=30,
    )
    grad_d, mixed_e, gi_d, go_e = call(
        decoder_back, meta, (5,),
        [
            fixed(mixed_d), fixed(codes), per_step(xh2_d), per_step(dg2_d), per_step(inv2_d), per_step(out_e),
            rows_chunk(cotangent_t),
        ]
        + halo + [per_step(xh3_e), per_step(dg3_e), per_step(inv3_e), per_step(third_e)]
        + w_conv + w_inner + w_outer + last_ins,
        [out_chunks(width, F32), out_fixed((rows, ext, LANES), BF), out_fixed((width, TILE)), out_fixed((width, TILE))],
        [
            scr((inner, 3 * inner), BF), scr((width, inner), BF), scr((inner, width), BF), pds(2), phs(2),
            scr((3 * inner, 2 * CHUNK), BF), hid_f, hid_b, hid_b, both_b, both_b, chunk_f, chunk_f, chunk_f, scr((2, 8, CHUNK), F32), pds(3), phs(6),
        ],
        name="decoder_back", us=40,
    )
    ins5 = (
        [
            fixed(mixed_e), fixed(sec_e), fixed(code_cols), per_step(xh2_e, 4), per_step(dg2_e, 4), per_step(inv2_e, 4),
            (tokens_t, pl.BlockSpec((2, width, CHUNK), lambda c, m: (m[0], 0, c))), per_step(grad_d, 4),
        ]
        + w_conv + w_inner + last_ins
        + [
            (flip(other_out, "pipe", 1), pl.BlockSpec((2, width, CHUNK), lambda c, m: (0, 0, c))),
            (mine_out, pl.BlockSpec(memory_space=pl.ANY)),
        ]
    )
    mine_grad, other_grad, gi_e, gc_e, section_output = call(
        encoder_back, meta, (4,), ins5,
        [
            (final[0], pl.BlockSpec((2, width, CHUNK), lambda c, m: (m[0], 0, c))),
            (sent[0], pl.BlockSpec((2, width, CHUNK), lambda c, m: (0, 0, c))),
            out_fixed((width, TILE)), out_fixed((5 * inner, TILE)),
            (final[0], pl.BlockSpec((2, width, CHUNK), lambda c, m: (1 - m[0], 0, c))),
        ],
        [
            scr((inner, 5 * LANES), BF), scr((width, inner), BF), pds(2), phs(1),
            scr((2 * CHUNK, 5 * LANES), BF), scr((2 * CHUNK, 5 * LANES), BF), scr((TILE, 5 * LANES), F32), hid_f, hid_b, both_b, chunk_f, chunk_f, chunk_f, scr((2, 8, CHUNK), F32), pds(2), phs(3),
        ],
        aliases={len(ins5): 4}, name="encoder_back", us=32,
    )

    def finish(mine, other):
        block = (1, width // 2, length)
        return jnp.transpose(
            call(
                fill_rows, meta, (2 * rows,),
                [
                    (flip(other, "pipe", 1), pl.BlockSpec(block, lambda c, m: (c // 2, c % 2, 0))),
                    (mine, pl.BlockSpec(memory_space=pl.ANY)),
                ],
                [(final[0], pl.BlockSpec(block, lambda c, m: (rows - rows * m[0] + c // 2, c % 2, 0)))],
                aliases={2: 0}, name="fill_rows", us=7,
            )[0],
            (0, 2, 1),
        )

    section_output = jnp.transpose(section_output, (0, 2, 1))[None]

    taps_rows = 4 * inner
    kept, sent = call(
        pack_grads, meta, (1,), [fixed(x) for x in (gi_e, go_e, gc_e, gi_d, go_d, gc_d)],
        [out_fixed((2 * width + taps_rows, TILE)), out_fixed((2 * width + taps_rows, TILE), BF)],
        name="pack_grads", us=4,
    )
    kept = kept + flip(sent, "pipe", 1).astype(F32)
    input_gradient = finish(mine_grad, other_grad)[None]
    parts, input_gradient = spread_over(kept, "seq", input_gradient)
    summed = collect_over(parts, "seq")
    grads_inner, grads_outer = summed[:width], summed[width : 2 * width]
    conv_sum = summed[2 * width :]
    conv_other = flip(conv_sum, "pipe", 1)
    summed_f = [x.astype(F32) for x in (grads_inner, grads_outer)]
    conv_first = jnp.where(encoder_side, conv_sum, conv_other)
    conv_second = jnp.where(encoder_side, conv_other, conv_sum)
    grad_conv_e = jnp.concatenate([conv_first, conv_second[:inner]], axis=0)[:, :loc].astype(F32).reshape(5, inner, loc)
    grad_conv_d = conv_second[inner:, :loc].astype(F32).reshape(3, inner, loc)
    grad_inner = summed_f[0][:, :loc]
    grad_outer = jnp.transpose(summed_f[1][:, :loc])
    wide = [summed_f[0][:, FREE], summed_f[0][:, FREE + 1], summed_f[1][:, FREE]]
    narrow = jnp.concatenate([summed_f[0][:inner, FREE + 2 : FREE + 5], summed_f[1][:inner, FREE + 1 : FREE + 4]], axis=1)
    narrow = jnp.transpose(lax.dynamic_slice_in_dim(narrow, tensor * loc, loc, 0))

    return (
        section_output,
        input_gradient,
        wide[0][None],
        wide[1][None],
        grad_inner[None],
        narrow[2][None],
        narrow[0][None],
        narrow[1][None],
        grad_conv_e,
        grad_conv_d,
        narrow[5][None],
        narrow[3][None],
        narrow[4][None],
        grad_outer[None],
        wide[2][None],
    )


def solution(mesh):
    return jax.shard_map(
        on_device,
        mesh=mesh,
        in_specs=(
            P(None, "seq", None),
            P(None, "seq"),
            P(None, "seq"),
            P(None, "seq", None),
            P("pipe", None),
            P("pipe", None),
            P("pipe", None, "tensor"),
            P("pipe", "tensor"),
            P("pipe", "tensor"),
            P("pipe", "tensor"),
            P(None, None, "tensor"),
            P(None, None, "tensor"),
            P("pipe", "tensor"),
            P("pipe", "tensor"),
            P("pipe", "tensor"),
            P("pipe", "tensor", None),
            P("pipe", None),
        ),
        out_specs=(
            P("pipe", None, "seq", None),
            P("pipe", None, "seq", None),
            P("pipe", None),
            P("pipe", None),
            P("pipe", None, "tensor"),
            P("pipe", "tensor"),
            P("pipe", "tensor"),
            P("pipe", "tensor"),
            P(None, None, "tensor"),
            P(None, None, "tensor"),
            P("pipe", "tensor"),
            P("pipe", "tensor"),
            P("pipe", "tensor"),
            P("pipe", "tensor", None),
            P("pipe", None),
        ),
        check_vma=False,
    )
```

```python
import functools
import math

import jax
import jax.numpy as jnp
from jax import lax
from jax.experimental import pallas as pl
from jax.experimental.pallas import tpu as pltpu
from jax.sharding import PartitionSpec as P

SPACING = 16
EPSILON = 1e-05
BF = jnp.bfloat16
F32 = jnp.float32
LANES = 512
TILE = 128
CHUNK = 256
BLOCK = 16
PIECE = 208
ROOT = math.sqrt(2.0 / math.pi)
CUBIC = 0.044715
E_OFFSETS = tuple(SPACING * (k - 2) for k in range(5))
D_OFFSETS = (-2, -1, 0)
VMEM = 60 * 1024 * 1024
FREE = 120
COT_TURNS = (96, 48)


def dot(a, b):
    return lax.dot_general(a, b, (((1,), (0,)), ((), ())), preferred_element_type=F32)


def dot_nt(a, b):
    return lax.dot_general(a, b, (((1,), (1,)), ((), ())), preferred_element_type=F32)


def pair(column):
    return jnp.concatenate([column, column], axis=1)


def row_sum(values):
    return jnp.sum(values, axis=0, keepdims=True)


def moments(get, count):
    total = square = None
    for j in range(0, count, BLOCK):
        x = get(j)
        total = x if total is None else total + x
        square = x * x if square is None else square + x * x
    center = row_sum(total) * (1.0 / count)
    inverse = lax.rsqrt(row_sum(square) * (1.0 / count) - center * center + EPSILON)
    return center * inverse, inverse


def gate(half):
    square = half * half
    return jnp.tanh(half * (2 * ROOT + (8 * CUBIC * ROOT) * square)), square


def slope(half, tanh, square):
    return (1.0 + tanh) * (0.5 + (half - half * tanh) * (ROOT + (12 * CUBIC * ROOT) * square))


def spread(target, source, columns, *whole):
    for n, c in enumerate(columns):
        value = jnp.broadcast_to(source[:, c : c + 1], target.shape[1:])
        target[n] = value if n in [w - 1 for w in whole] else 0.5 * value


def param(ref, n, j):
    return pair(ref[n, j : j + BLOCK, :])


def placed(sel, a_ref, b_ref, lo):
    parts = []
    for q in range(a_ref.shape[0]):
        part = jnp.where(sel, a_ref[q, lo : lo + PIECE, :], b_ref[q, lo : lo + PIECE, :])
        parts.append(part.astype(F32)[:200])
    return jnp.concatenate(parts, axis=0).astype(BF)


def tap_of(sel, a_ref, b_ref, tap, inner):
    q = tap % 4
    first, second = a_ref[q, :inner, :], b_ref[q, :inner, :]
    return jnp.where(sel, first, second) if tap < 4 else jnp.where(sel, second, first)


def drive(live, *streams):
    def stage(fn):
        @pl.when(live)
        def _():
            fn()

    count = max(len(x) for x in streams)
    for slot in range(count + 1):
        here = [s[slot - n] for n, s in enumerate(streams) if 0 <= slot - n < len(s)]
        if slot % 2 == 0:
            here.reverse()
        stage(lambda here=here: [fn() for fn in here])


def tiles_of(step):
    return jnp.where(step == 0, 1, 2 * step), jnp.where(step == 0, 10, 2 * step + 1)


def at_tile(a, count=1):
    return pl.ds(pl.multiple_of(a * TILE, TILE), count * TILE)


def code_rows(code_ref, n, a, offsets):
    window = code_ref[n, :, at_tile(a - 1, 3)]
    here = window[:, TILE : 2 * TILE]
    return [(window[:, TILE + o : 2 * TILE + o] == here).astype(F32) for o in offsets], (here > 0.5).astype(F32)


def taps(cat_ref, ref, code_ref, n, step, offsets, count):
    kept = []
    for half, a in enumerate(tiles_of(step)):
        masks, keep = code_rows(code_ref, n, a, offsets)
        kept.append(keep)
        lanes = slice(n * CHUNK + half * TILE, n * CHUNK + (half + 1) * TILE)
        window = ref[n, :, at_tile(a - 1, 3)]
        for k, offset in enumerate(offsets):
            piece = window[:, TILE + offset : 2 * TILE + offset]
            if offset:
                piece = piece * masks[k].astype(BF)
            cat_ref[k * count : (k + 1) * count, lanes] = piece
    return jnp.concatenate(kept, axis=1)


def row_taps(cat_ref, ref, col_ref, n, step, offsets):
    for half, a in enumerate(tiles_of(step)):
        here = col_ref[n, at_tile(a), :]
        rows = slice(n * CHUNK + half * TILE, n * CHUNK + (half + 1) * TILE)
        for k, offset in enumerate(offsets):
            there = pl.ds(pl.multiple_of(a * TILE + offset, BLOCK), TILE)
            piece = ref[n, there, :]
            if offset:
                mask = (col_ref[n, there, :] == here).astype(BF)
                piece = piece * jnp.concatenate([mask] * (LANES // TILE), axis=1)
            cat_ref[rows, k * LANES : (k + 1) * LANES] = piece


def put_rows(ext_ref, n, step, values):
    turned = jnp.transpose(values[...])
    for half, a in enumerate(tiles_of(step)):
        ext_ref[n, at_tile(a), 0 : turned.shape[1]] = turned[half * TILE : (half + 1) * TILE, :]


def keep_row(code_ref, n, step):
    return jnp.concatenate([(code_ref[n, :, at_tile(a)] > 0.5).astype(F32) for a in tiles_of(step)], axis=1)


def put(ext_ref, n, step, values):
    for half, a in enumerate(tiles_of(step)):
        ext_ref[n, :, at_tile(a)] = values[:, half * TILE : (half + 1) * TILE]


def blank_ends(ext_ref):
    for a in (0, 11):
        ext_ref[:, :, a * TILE : (a + 1) * TILE] = jnp.zeros(ext_ref.shape[:2] + (TILE,), BF)


def from_sums(total, square, count):
    center = row_sum(total) * (1.0 / count)
    inverse = lax.rsqrt(row_sum(square) * (1.0 / count) - center * center + EPSILON)
    return center * inverse, inverse


def biased(hid_ref, ph, n):
    count = hid_ref.shape[0]
    total = square = None
    for j in range(0, count, BLOCK):
        x = hid_ref[j : j + BLOCK, :] + param(ph, n, j)
        hid_ref[j : j + BLOCK, :] = x
        total = x if total is None else total + x
        square = x * x if square is None else square + x * x
    return from_sums(total, square, count)


def activate(hid_ref, stats, ph, gain, bias, out_ref, xh_ref, dg_ref, inv_ref):
    shift, inverse = stats
    inv_ref[...] = jnp.broadcast_to(inverse, inv_ref.shape)
    for j in range(0, hid_ref.shape[0], BLOCK):
        scaled = hid_ref[j : j + BLOCK, :] * inverse - shift
        half = scaled * param(ph, gain, j) + param(ph, bias, j)
        tanh, square = gate(half)
        out_ref[j : j + BLOCK, :] = (half + half * tanh).astype(BF)
        xh_ref[j : j + BLOCK, :] = scaled.astype(BF)
        dg_ref[j : j + BLOCK, :] = slope(half, tanh, square).astype(BF)


def first_of(x_ref, stats, pd, gain, out_ref, slope_ref=None, scaled_ref=None):
    shift, inverse = stats
    for j in range(0, x_ref.shape[0], BLOCK):
        scaled = x_ref[j : j + BLOCK, :] * inverse - shift
        half = scaled * param(pd, gain, j) + param(pd, gain + 1, j)
        tanh, square = gate(half)
        out_ref[j : j + BLOCK, :] = (half + half * tanh).astype(BF)
        if slope_ref is not None:
            slope_ref[j : j + BLOCK, :] = slope(half, tanh, square)
            scaled_ref[j : j + BLOCK, :] = scaled


def moments_of(x_ref):
    return moments(lambda j: x_ref[j : j + BLOCK, :], x_ref.shape[0])


def halves(values):
    return values[:, :TILE] + values[:, TILE:]


def norm_back(grad_ref, xh_ref, dg_ref, inverse, ph, gain, low_ref, acc, base):
    count = low_ref.shape[0]
    first = second = None
    for j in range(0, count, BLOCK):
        down = grad_ref[j : j + BLOCK, :] * dg_ref[j : j + BLOCK, :].astype(F32)
        cross = down * xh_ref[j : j + BLOCK, :].astype(F32)
        acc[base, j : j + BLOCK, :] += halves(cross)
        acc[base + 1, j : j + BLOCK, :] += halves(down)
        g = param(ph, gain, j)
        weighted = down * g
        grad_ref[j : j + BLOCK, :] = weighted
        first = weighted if first is None else first + weighted
        second = cross * g if second is None else second + cross * g
    twice = inverse * 2.0
    first = row_sum(first) * (twice * (1.0 / count))
    second = row_sum(second) * (twice * (1.0 / count))
    for j in range(0, count, BLOCK):
        result = grad_ref[j : j + BLOCK, :] * twice - first - xh_ref[j : j + BLOCK, :].astype(F32) * second
        low_ref[j : j + BLOCK, :] = result.astype(BF)
        acc[base + 2, j : j + BLOCK, :] += halves(result)


def own_rows(pick_ref, values):
    return dot(pick_ref[...], values).astype(BF)


def columns(target, lane, acc, order):
    count = acc.shape[1]
    for n, k in enumerate(order):
        target[0:count, lane + n : lane + n + 1] = jnp.sum(acc[k], axis=1, keepdims=True)


def clear(step, *refs):
    @pl.when(step <= 1)
    def _():
        for ref in refs:
            ref[...] = jnp.zeros_like(ref)


def turned(tile, by):
    return pltpu.roll(tile, by, 1) if by else tile


def fetch(step, target, own_ref, before_ref, after_ref, turns):
    @pl.when(step == 0)
    def _():
        width = target.shape[1]
        for n in range(2):
            target[n, :, 0:TILE] = turned(before_ref[n, 0:width, :].astype(F32), turns[0])
            target[n, :, TILE:] = turned(after_ref[n, 0:width, :].astype(F32), turns[1])

    @pl.when(step > 0)
    def _():
        target[...] = own_ref[...]


def encoder_in(meta, tok_ref, before_ref, after_ref, a_ref, b_ref, eye_ref, pd_ref, ph_ref,
               sec_ref, xh_ref, dg_ref, inv_ref, wi, pd, ph, x_s, first_s, hid_s, sec_s):
    step = pl.program_id(0)

    @pl.when(step == 0)
    def _():
        spread(pd, pd_ref, (0, 1))
        spread(ph, ph_ref, (0, 1, 2), 1)
        wi[...] = dot_nt(eye_ref[...], placed(meta[0] == 0, a_ref, b_ref, 0)).astype(BF)
        sec_ref[...] = jnp.zeros_like(sec_ref)

    fetch(step, x_s, tok_ref, before_ref, after_ref, (0, 0))

    def stream(n):
        def enter():
            first_of(x_s.at[n], moments_of(x_s.at[n]), pd, 0, first_s.at[n])

        def product():
            hid_s[n] = dot(wi[...], first_s[n])

        def leave():
            stats = biased(hid_s.at[n], ph, 0)
            activate(hid_s.at[n], stats, ph, 1, 2, sec_s.at[n], xh_ref.at[n], dg_ref.at[n], inv_ref.at[n])
            put_rows(sec_ref, n, step, sec_s.at[n])

        return [enter, product, leave]

    drive(meta[0] >= 0, stream(0), stream(1))


def encoder_out(meta, sec_ref, code_ref, col_ref, tok_ref, before_ref, after_ref, a_ref, b_ref, ao_ref, bo_ref, ai_ref, bi_ref,
                eye_ref, pick_ref, pd_ref, ph_ref,
                out_ref, xh3_ref, dg3_ref, inv3_ref, third_ref, secd_ref, xh2_ref, dg2_ref, inv2_ref,
                wc, wo, wi, pd, ph, cat, hid_s, third_s, first_s, sec_s, wide_s):
    step = pl.program_id(0)
    width = tok_ref.shape[1]
    inner = eye_ref.shape[0]

    @pl.when(step == 0)
    def _():
        spread(pd, pd_ref, (2, 3, 4), 1)
        spread(ph, ph_ref, (3, 4, 5, 6, 7, 8), 1, 4)
        sel = meta[0] == 0
        wc[...] = jnp.zeros_like(wc)
        for k in range(5):
            wc[:, k * LANES : k * LANES + inner] = dot_nt(eye_ref[...], tap_of(sel, a_ref, b_ref, k, inner)).astype(BF)
        wo[...] = dot_nt(placed(sel, ao_ref, bo_ref, 0), eye_ref[...]).astype(BF)
        wi[...] = dot_nt(eye_ref[...], placed(sel, bi_ref, ai_ref, 0)).astype(BF)
        blank_ends(secd_ref)

    fetch(step, out_ref, tok_ref, before_ref, after_ref, (0, 0))

    def stream(n):
        rows = slice(n * CHUNK, (n + 1) * CHUNK)

        def sources():
            row_taps(cat, sec_ref, col_ref, n, step, E_OFFSETS)

        def convolve():
            hid_s[n] = dot_nt(wc[...], cat[rows, :])

        def activate3():
            stats = biased(hid_s.at[n], ph, 0)
            activate(hid_s.at[n], stats, ph, 1, 2, third_s.at[n], xh3_ref.at[n], dg3_ref.at[n], inv3_ref.at[n])

        def project():
            wide_s[n] = dot(wo[...], third_s[n])
            third_ref[n] = own_rows(pick_ref, third_s[n])

        def add():
            kept = jnp.broadcast_to(keep_row(code_ref, n, step), (BLOCK, CHUNK))
            total = square = None
            for j in range(0, width, BLOCK):
                x = out_ref[n, j : j + BLOCK, :] + kept * (wide_s[n, j : j + BLOCK, :] + param(pd, 0, j))
                out_ref[n, j : j + BLOCK, :] = x
                total = x if total is None else total + x
                square = x * x if square is None else square + x * x
            first_of(out_ref.at[n], from_sums(total, square, width), pd, 1, first_s.at[n])

        def product():
            hid_s[n] = dot(wi[...], first_s[n])

        def leave():
            stats = biased(hid_s.at[n], ph, 3)
            activate(hid_s.at[n], stats, ph, 4, 5, sec_s.at[n], xh2_ref.at[n], dg2_ref.at[n], inv2_ref.at[n])
            put(secd_ref, n, step, sec_s.at[n])

        return [sources, convolve, activate3, project, add, product, leave]

    drive(meta[0] >= 0, stream(0), stream(1))


def decoder_out(meta, sec_ref, code_ref, in_ref, cot_ref, before_ref, after_ref, a_ref, b_ref, ao_ref, bo_ref, eye_ref, pick_ref,
                pd_ref, ph_ref,
                mine_ref, other_ref, mixed_ref, go_ref, gc_ref,
                wc, wo, wob, pd, ph, cat, hid_s, third_s, cot_f, cot_s, low_s, xh_s, dg_s, inv_s, grad_s, accd, acch):
    step = pl.program_id(0)
    width = in_ref.shape[1]
    inner = eye_ref.shape[0]

    @pl.when(step == 0)
    def _():
        spread(pd, pd_ref, (5,), 1)
        spread(ph, ph_ref, (9, 10, 11), 1)
        sel = meta[0] == 0
        for k in range(3):
            wc[:, k * inner : (k + 1) * inner] = dot_nt(eye_ref[...], tap_of(sel, a_ref, b_ref, 5 + k, inner)).astype(BF)
        outer = placed(sel, bo_ref, ao_ref, 0)
        wo[...] = dot_nt(outer, eye_ref[...]).astype(BF)
        wob[...] = dot_nt(eye_ref[...], outer).astype(BF)
        blank_ends(mixed_ref)

    clear(step, go_ref, gc_ref, accd, acch)
    fetch(step, cot_f, cot_ref, before_ref, after_ref, COT_TURNS)
    encoder_side = meta[0] == 0

    def stream(n):
        lanes = slice(n * CHUNK, (n + 1) * CHUNK)

        def sources():
            kept = jnp.broadcast_to(keep_row(code_ref, n, step), (BLOCK, CHUNK))
            for j in range(0, width, BLOCK):
                branch = kept * cot_f[n, j : j + BLOCK, :]
                accd[0, j : j + BLOCK, :] += halves(branch)
                cot_s[j : j + BLOCK, lanes] = branch.astype(BF)
            taps(cat, sec_ref, code_ref, n, step, D_OFFSETS, inner)

        def convolve():
            hid_s[n] = dot(wc[...], cat[:, lanes])
            grad_s[n] = dot(wob[...], cot_s[:, lanes])

        def middle():
            stats = biased(hid_s.at[n], ph, 0)
            activate(hid_s.at[n], stats, ph, 1, 2, third_s.at[n], xh_s.at[n], dg_s.at[n], inv_s.at[n])
            norm_back(grad_s.at[n], xh_s.at[n], dg_s.at[n], stats[1], ph, 1, low_s.at[n], acch, 0)
            put(mixed_ref, n, step, low_s.at[n])

        def project():
            cot_f[n] = dot(wo[...], third_s[n])

        def add():
            kept = jnp.broadcast_to(keep_row(code_ref, n, step), (BLOCK, CHUNK))
            for j in range(0, width, BLOCK):
                x = in_ref[n, j : j + BLOCK, :]
                y = x + kept * (cot_f[n, j : j + BLOCK, :] + param(pd, 0, j))
                mine_ref[n, j : j + BLOCK, :] = jnp.where(encoder_side, x, y)
                other_ref[n, j : j + BLOCK, :] = jnp.where(encoder_side, y, x).astype(BF)

        return [sources, convolve, middle, project, add]

    def weights():
        picked = own_rows(pick_ref, jnp.concatenate([third_s[0], third_s[1], low_s[0], low_s[1]], axis=1))
        go_ref[...] += dot_nt(cot_s[...], picked[:, : 2 * CHUNK])
        gc_ref[...] += dot_nt(cat[...], picked[:, 2 * CHUNK :])

    drive(meta[0] >= 0, stream(0) + [weights], stream(1))

    @pl.when(step == 4)
    def _():
        columns(go_ref, FREE, accd, (0,))
        columns(go_ref, FREE + 1, acch, (0, 1, 2))


def input_back(wide_ref, scaled_ref, inverse, dg1_ref, pd, accd, finish):
    width = wide_ref.shape[0]
    first = second = None
    for j in range(0, width, BLOCK):
        scaled = scaled_ref[j : j + BLOCK, :]
        down = wide_ref[j : j + BLOCK, :] * dg1_ref[j : j + BLOCK, :]
        cross = down * scaled
        accd[0, j : j + BLOCK, :] += halves(cross)
        accd[1, j : j + BLOCK, :] += halves(down)
        g = param(pd, 0, j)
        weighted = down * g
        wide_ref[j : j + BLOCK, :] = weighted
        first = weighted if first is None else first + weighted
        second = cross * g if second is None else second + cross * g
    twice = inverse * 2.0
    first = row_sum(first) * (twice * (1.0 / width))
    second = row_sum(second) * (twice * (1.0 / width))
    for j in range(0, width, BLOCK):
        finish(j, wide_ref[j : j + BLOCK, :] * twice - first - scaled_ref[j : j + BLOCK, :] * second)


def decoder_back(meta, mixed_ref, code_ref, xh2_ref, dg2_ref, inv2_ref, in_ref, cot_ref, before_ref, after_ref,
                 xh3_ref, dg3_ref, inv3_ref, third_ref, a_ref, b_ref, ai_ref, bi_ref, ao_ref, bo_ref, eye_ref, pick_ref,
                 pd_ref, ph_ref,
                 grad_ref, low3_ref, gi_ref, go_ref,
                 wc, wib, wob, pd, ph, cat, hid_s, low_s, low3_s, first_s, branch_s, dg1_s, wide_s, scaled_s, inv1_s, accd, acch):
    step = pl.program_id(0)
    inner = eye_ref.shape[0]

    @pl.when(step == 0)
    def _():
        spread(pd, pd_ref, (3, 4))
        spread(ph, ph_ref, (7, 4))
        sel = meta[0] == 0
        for k in range(3):
            wc[:, k * inner : (k + 1) * inner] = dot_nt(tap_of(sel, a_ref, b_ref, 5 + k, inner), eye_ref[...]).astype(BF)
        wib[...] = dot_nt(placed(sel, bi_ref, ai_ref, 0), eye_ref[...]).astype(BF)
        wob[...] = dot_nt(eye_ref[...], placed(sel, ao_ref, bo_ref, 0)).astype(BF)
        low3_ref[...] = jnp.zeros_like(low3_ref)

    clear(step, gi_ref, go_ref, accd, acch)
    fetch(step, grad_ref, cot_ref, before_ref, after_ref, COT_TURNS)

    def stream(n):
        lanes = slice(n * CHUNK, (n + 1) * CHUNK)

        def sources():
            taps(cat, mixed_ref, code_ref, n, step, tuple(-o for o in D_OFFSETS), inner)
            stats = moments_of(in_ref.at[n])
            inv1_s[n] = jnp.broadcast_to(stats[1], inv1_s.shape[1:])
            first_of(in_ref.at[n], stats, pd, 0, first_s.at[:, lanes], dg1_s.at[n], scaled_s.at[n])

        def convolve():
            hid_s[n] = dot(wc[...], cat[:, lanes])

        def second():
            norm_back(hid_s.at[n], xh2_ref.at[n], dg2_ref.at[n], inv2_ref[n, 0:1, :], ph, 0, low_s.at[n], acch, 0)

        def project():
            wide_s[n] = dot(wib[...], low_s[n])

        def leave():
            kept = jnp.broadcast_to(keep_row(code_ref, n, step), (BLOCK, CHUNK))

            def finish(j, value):
                value = grad_ref[n, j : j + BLOCK, :] + value
                grad_ref[n, j : j + BLOCK, :] = value
                branch = kept * value
                accd[2, j : j + BLOCK, :] += halves(branch)
                branch_s[j : j + BLOCK, lanes] = branch.astype(BF)

            input_back(wide_s.at[n], scaled_s.at[n], inv1_s[n, 0:1, :], dg1_s.at[n], pd, accd, finish)

        def outward():
            hid_s[n] = dot(wob[...], branch_s[:, lanes])

        def third():
            norm_back(hid_s.at[n], xh3_ref.at[n], dg3_ref.at[n], inv3_ref[n, 0:1, :], ph, 1, low3_s.at[n], acch, 3)
            put_rows(low3_ref, n, step, low3_s.at[n])

        return [sources, convolve, second, project, leave, outward, third]

    def weights():
        low = own_rows(pick_ref, jnp.concatenate([low_s[0], low_s[1]], axis=1))
        third = jnp.concatenate([third_ref[n] for n in range(2)], axis=1)
        gi_ref[...] += dot_nt(first_s[...], low)
        go_ref[...] += dot_nt(branch_s[...], third)

    drive(meta[0] >= 0, stream(0) + [weights], stream(1))

    @pl.when(step == 4)
    def _():
        columns(gi_ref, FREE, accd, (0, 1))
        columns(gi_ref, FREE + 2, acch, (0, 1, 2))
        columns(go_ref, FREE, accd, (2,))
        columns(go_ref, FREE + 1, acch, (3, 4, 5))


def encoder_back(meta, mixed_ref, sec_ref, col_ref, xh2_ref, dg2_ref, inv2_ref, in_ref, later_ref, a_ref, b_ref,
                 ai_ref, bi_ref, eye_ref, pick_ref, pd_ref, ph_ref, recv_ref, goe, gid, god, gcd, final_ref,
                 mine_ref, other_ref, kept_ref, sent_ref, out_ref,
                 wc, wib, pd, ph, cat, catw, gc_s, hid_s, low_s, first_s, dg1_s, wide_s, scaled_s, inv1_s, gi_ref, accd, acch):
    del final_ref
    step = pl.program_id(0) + 1
    inner = eye_ref.shape[0]

    @pl.when(step == 1)
    def _():
        spread(pd, pd_ref, (0, 1))
        spread(ph, ph_ref, (1,))
        sel = meta[0] == 0
        wc[...] = jnp.zeros_like(wc)
        for k in range(5):
            wc[:, k * LANES : k * LANES + inner] = dot_nt(tap_of(sel, a_ref, b_ref, k, inner), eye_ref[...]).astype(BF)
        wib[...] = dot_nt(placed(sel, ai_ref, bi_ref, 0), eye_ref[...]).astype(BF)

    clear(step, gi_ref, gc_s, accd, acch)
    encoder_side = meta[0] == 0

    def stream(n):
        lanes = slice(n * CHUNK, (n + 1) * CHUNK)

        def sources():
            out_ref[n] = recv_ref[n].astype(F32)
            row_taps(cat, mixed_ref, col_ref, n, step, tuple(-o for o in E_OFFSETS))
            row_taps(catw, sec_ref, col_ref, n, step, E_OFFSETS)
            stats = moments_of(in_ref.at[n])
            inv1_s[n] = jnp.broadcast_to(stats[1], inv1_s.shape[1:])
            first_of(in_ref.at[n], stats, pd, 0, first_s.at[:, lanes], dg1_s.at[n], scaled_s.at[n])

        def convolve():
            hid_s[n] = dot_nt(wc[...], cat[lanes, :])

        def second():
            norm_back(hid_s.at[n], xh2_ref.at[n], dg2_ref.at[n], inv2_ref[n, 0:1, :], ph, 0, low_s.at[n], acch, 0)

        def project():
            wide_s[n] = dot(wib[...], low_s[n])
            if n:
                mixed = [
                    dot_nt(pick_ref[...], mixed_ref[r, at_tile(2 * step, 2), 0:inner]).astype(BF) for r in range(2)
                ]
                gc_s[...] += dot(jnp.concatenate(mixed, axis=1), catw[...])

        def leave():
            def finish(j, value):
                later = later_ref[n, j : j + BLOCK, :]
                value = later + value
                mine_ref[n, j : j + BLOCK, :] = jnp.where(encoder_side, value, later)
                other_ref[n, j : j + BLOCK, :] = jnp.where(encoder_side, later, value).astype(BF)

            input_back(wide_s.at[n], scaled_s.at[n], inv1_s[n, 0:1, :], dg1_s.at[n], pd, accd, finish)

        return [sources, convolve, second, project, leave]

    def weights():
        low = own_rows(pick_ref, jnp.concatenate([low_s[0], low_s[1]], axis=1))
        gi_ref[...] += dot_nt(first_s[...], low)

    drive(meta[0] >= 0, stream(0) + [weights], stream(1))

    @pl.when(step == 4)
    def _():
        columns(gi_ref, FREE, accd, (0, 1))
        columns(gi_ref, FREE + 2, acch, (0, 1, 2))
        gce = [jnp.transpose(gc_s[:, k * LANES : k * LANES + inner]) for k in range(5)]
        pieces = [(gi_ref[...], gid[...]), (goe[...], god[...]), (gce[0], gce[4])]
        pieces += [(gce[k], gcd[(k - 1) * inner : k * inner, :]) for k in range(1, 4)]
        start = 0
        for e, d in pieces:
            rows = slice(start, start + e.shape[0])
            start += e.shape[0]
            kept_ref[rows, :] = jnp.where(encoder_side, e, d)
            sent_ref[rows, :] = jnp.where(encoder_side, d, e).astype(BF)


def fill_rows(meta, recv_ref, final_ref, out_ref):
    del meta, final_ref
    out_ref[...] = recv_ref[...].astype(F32)


def pack_edges(meta, tok_last, cot_last, tok_first, cot_first, code_last, code_first, tail_ref, head_ref):
    del meta
    width = tok_last.shape[1]
    lane = lax.broadcasted_iota(jnp.int32, (width, TILE), 1)
    for n in range(2):
        tail_ref[n, 0:width, :] = jnp.where(lane < 32, turned(cot_last[n], 32), tok_last[n]).astype(BF)
        head_ref[n, 0:width, :] = jnp.where(lane < 80, tok_first[n], turned(cot_first[n], 80)).astype(BF)
        tail_ref[n, width:, :] = jnp.broadcast_to(code_last[n], (BLOCK, TILE)).astype(BF)
        head_ref[n, width:, :] = jnp.broadcast_to(code_first[n], (BLOCK, TILE)).astype(BF)


def place_weights(place, own_ref, *refs):
    out_ref = refs[-1]
    for q in range(4):
        out_ref[q, :, at_tile(place[1])] = own_ref[q]
    for by in range(4):
        for slot in range(1, 4):
            out_ref[place[0] ^ by, :, at_tile(place[1] ^ slot)] = refs[by][slot - 1]


def call(body, meta, grid, ins, outs, scratch=(), aliases=None, name=None, us=3):
    return pl.pallas_call(
        body,
        grid_spec=pltpu.PrefetchScalarGridSpec(
            num_scalar_prefetch=1,
            grid=grid,
            in_specs=[s for _, s in ins],
            out_specs=[s for _, s in outs],
            scratch_shapes=list(scratch),
        ),
        out_shape=[s for s, _ in outs],
        input_output_aliases=aliases or {},
        compiler_params=pltpu.CompilerParams(
            dimension_semantics=("arbitrary",) * len(grid), vmem_limit_bytes=VMEM
        ),
        cost_estimate=pl.CostEstimate(flops=int(us * 1.0e9), bytes_accessed=int(us * 3.5e6), transcendentals=0),
        name=name,
    )(meta, *[a for a, _ in ins])


def per_step(array, steps=5):
    first = array.shape[0] // 2 - steps
    return (array, pl.BlockSpec((2,) + array.shape[1:], lambda c, m: (c + first, 0, 0)))


def own_index(c, m):
    return (m[0], 0, jnp.maximum(c - 1, 0))


def rows_chunk(array):
    return (array, pl.BlockSpec((2, array.shape[1], CHUNK), own_index))


def fixed(array):
    zeros = (0,) * array.ndim
    return (array, pl.BlockSpec(array.shape, lambda c, m: zeros))


def part(array, rows, index):
    return (array, pl.BlockSpec((array.shape[0], rows, array.shape[2]), lambda c, m: (0, index, 0)))


def out_chunks(rows, dtype):
    return (jax.ShapeDtypeStruct((10, rows, CHUNK), dtype), pl.BlockSpec((2, rows, CHUNK), lambda c, m: (c, 0, 0)))


def out_fixed(shape, dtype=F32):
    zeros = (0,) * len(shape)
    return (jax.ShapeDtypeStruct(shape, dtype), pl.BlockSpec(shape, lambda c, m: zeros))


def flip(x, axis, by):
    count = lax.axis_size(axis)
    return lax.ppermute(x, axis, [(i, i ^ by) for i in range(count)])


def gather(x, axis):
    me = lax.axis_index(axis)
    count = lax.axis_size(axis)
    result = jnp.zeros((count,) + x.shape, x.dtype)
    result = lax.dynamic_update_index_in_dim(result, x, me, 0)
    for by in range(1, count):
        result = lax.dynamic_update_index_in_dim(result, flip(x, axis, by), me ^ by, 0)
    return result


def gather_lanes(x, axis):
    me = lax.axis_index(axis)
    count = lax.axis_size(axis)
    lanes = x.shape[-1]
    result = jnp.zeros(x.shape[:-1] + (count * lanes,), x.dtype)
    result = lax.dynamic_update_slice_in_dim(result, x, me * lanes, 1)
    for by in range(1, count):
        result = lax.dynamic_update_slice_in_dim(result, flip(x, axis, by), (me ^ by) * lanes, 1)
    return result


def spread_over(x, axis, beside):
    count = lax.axis_size(axis)
    me = lax.axis_index(axis)
    parts = x.reshape((count, x.shape[0] // count) + x.shape[1:])
    low = parts.astype(BF)
    arrived = [
        flip(lax.dynamic_index_in_dim(low, me ^ by, 0, keepdims=False), axis, by) for by in range(1, count)
    ]
    arrived, beside = lax.optimization_barrier((arrived, beside))
    total = lax.dynamic_index_in_dim(parts, me, 0, keepdims=False)
    for part_of in arrived:
        total = total + part_of.astype(F32)
    return total.astype(BF), beside


def collect_over(x, axis):
    me = lax.axis_index(axis)
    count = lax.axis_size(axis)
    arrived = [flip(x, axis, by) for by in range(1, count)]
    result = jnp.zeros((count,) + x.shape, x.dtype)
    result = lax.dynamic_update_index_in_dim(result, x, me, 0)
    for by in range(1, count):
        result = lax.dynamic_update_index_in_dim(result, arrived[by - 1], me ^ by, 0)
    return result.reshape((count * x.shape[0],) + x.shape[1:])


def pad_to(x, axis, size):
    widths = [(0, 0)] * x.ndim
    widths[axis] = (0, size - x.shape[axis])
    return jnp.pad(x, widths)


def on_device(
    tokens, segments, pad_mask, cotangent, gain_first, bias_first, weight_inner, bias_inner, gain_middle, bias_middle,
    weight_conv_encoder, weight_conv_decoder, bias_conv, gain_last, bias_last, weight_outer, bias_outer,
):
    pipe, seq, tensor = (lax.axis_index(a) for a in ("pipe", "seq", "tensor"))
    n_pipe, n_seq, n_tensor = (lax.axis_size(a) for a in ("pipe", "seq", "tensor"))
    rows_all, length, width = tokens.shape
    rows = rows_all // n_pipe
    loc = weight_conv_encoder.shape[2]
    inner = weight_conv_encoder.shape[1]
    lanes = LANES // n_tensor
    encoder_side = pipe == 0
    meta = jnp.stack([pipe, tensor * loc]).astype(jnp.int32)
    tokens_t, cotangent_t = jnp.transpose(tokens, (0, 2, 1)), jnp.transpose(cotangent, (0, 2, 1))

    def mine_rows(array):
        return lax.dynamic_slice_in_dim(array, pipe * rows, rows, 0)

    codes = (mine_rows(jnp.where(pad_mask == 1, segments + 1, 0)).astype(F32) + 1.0)[:, None, :]
    last = length // TILE - 1

    def edge_tile(array, row, index):
        return (array, pl.BlockSpec((2, array.shape[1], TILE), lambda c, m: (m[0] if row else 0, 0, index)))

    edge_out = out_fixed((rows, width + BLOCK, TILE), BF)
    tail, head = call(
        pack_edges, meta, (1,),
        [
            edge_tile(tokens_t, True, last), edge_tile(cotangent_t, True, last),
            edge_tile(tokens_t, True, 0), edge_tile(cotangent_t, True, 0),
            edge_tile(codes, False, last), edge_tile(codes, False, 0),
        ],
        [edge_out, edge_out], name="pack_edges", us=4,
    )

    small = jnp.stack([bias_inner[0], gain_middle[0], bias_middle[0], bias_conv[0], gain_last[0], bias_last[0]])
    high = lax.reduce_precision(small, 8, 7)
    small = pad_to(jnp.concatenate([high, small - high], axis=0), 0, BLOCK)
    inner_all = pad_to(weight_inner[0].reshape(n_seq, width // n_seq, loc), 1, PIECE)
    inner_all = jnp.concatenate([inner_all, jnp.broadcast_to(small[None], (n_seq,) + small.shape)], axis=1)
    outer_all = pad_to(jnp.transpose(weight_outer[0]).reshape(n_seq, width // n_seq, loc), 1, PIECE)
    conv_all = pad_to(
        jnp.where(
            encoder_side,
            weight_conv_encoder[:4],
            jnp.concatenate([weight_conv_encoder[4:], weight_conv_decoder], axis=0),
        ), 1, 2 * PIECE,
    )

    def gathered(pieces, ahead=None, between=None):
        pieces = pad_to(pieces.astype(BF), 2, lanes)
        sent = lax.dynamic_index_in_dim(pieces, seq, 0, keepdims=False)
        if ahead is not None:
            sent, _ = lax.optimization_barrier((sent, ahead))
        if lanes != TILE or n_seq != 4:
            return gather(gather_lanes(sent, "tensor"), "seq")
        near = jnp.stack([flip(sent, "tensor", by) for by in range(1, 4)])
        if between is not None:
            near, _ = lax.optimization_barrier((near, between))
        return [pieces, near] + [flip(near, "seq", by) for by in range(1, 4)]

    def placed_parts(parts):
        if not isinstance(parts, list):
            return parts
        rows_in = parts[0].shape[1]
        return call(
            place_weights, jnp.stack([seq, tensor]).astype(jnp.int32), (1,), [fixed(x) for x in parts],
            [out_fixed((4, rows_in, LANES), BF)], name="place_weights", us=4,
        )[0]

    before = lax.ppermute(tail, "seq", [(i, i + 1) for i in range(n_seq - 1)])
    after = lax.ppermute(head, "seq", [(i + 1, i) for i in range(n_seq - 1)])
    parts1 = gathered(inner_all)
    parts2 = gathered(jnp.concatenate([conv_all, outer_all], axis=1), (tail, head))
    parts1, before, after = lax.optimization_barrier((parts1, before, after))
    bundle1 = placed_parts(parts1)
    large = jnp.stack([gain_first[0], bias_first[0], bias_outer[0]], axis=0)
    bundle1b, large2 = flip(bundle1, "pipe", 1), flip(large, "pipe", 1)
    def columns_of(mine, other):
        first, second = jnp.where(encoder_side, mine, other), jnp.where(encoder_side, other, mine)
        return pad_to(jnp.transpose(jnp.concatenate([first, second], axis=0)), 1, TILE)

    def small_of(bundle):
        values = bundle[0, PIECE : PIECE + 12].astype(F32)
        values = (values[:6] + values[6:]).reshape(6, n_tensor, lanes)
        return values[:, :, :loc].reshape(6, inner)

    ph, pd = columns_of(small_of(bundle1), small_of(bundle1b)), columns_of(large, large2)
    first_lane = jnp.arange(inner)
    first_lane = first_lane // loc * lanes + first_lane % loc
    eye = (first_lane[:, None] == jnp.arange(LANES)[None, :]).astype(BF)
    own = (jnp.arange(TILE)[:, None] + tensor * loc == jnp.arange(inner)[None, :]) & (jnp.arange(TILE)[:, None] < loc)
    own = own.astype(BF)
    w_inner = [part(bundle1, PIECE + BLOCK, 0), part(bundle1b, PIECE + BLOCK, 0)]
    none = jnp.zeros((rows, 1, TILE), F32)
    codes = jnp.concatenate(
        [none, before[:, width : width + 1].astype(F32), codes, after[:, width : width + 1].astype(F32), none], axis=2
    ) - 1.0
    code_cols = jnp.broadcast_to(codes[:, 0, :, None], (rows, codes.shape[2], TILE)).astype(BF)
    halo = [fixed(before), fixed(after)]

    ext = length + 4 * TILE
    scr = pltpu.VMEM
    chunk_f = scr((2, width, CHUNK), F32)
    chunk_b = scr((2, width, CHUNK), BF)
    both_b = scr((width, 2 * CHUNK), BF)
    hid_f = scr((2, inner, CHUNK), F32)
    hid_b = scr((2, inner, CHUNK), BF)

    def pds(n):
        return scr((n, width, TILE), F32)

    def phs(n):
        return scr((n, inner, TILE), F32)

    last_ins = [fixed(eye), fixed(own), fixed(pd), fixed(ph)]
    sec_e, xh2_e, dg2_e, inv2_e = call(
        encoder_in, meta, (5,),
        [rows_chunk(tokens_t)] + halo + w_inner + [fixed(eye), fixed(pd), fixed(ph)],
        [out_fixed((rows, ext, LANES), BF), out_chunks(inner, BF), out_chunks(inner, BF), out_chunks(8, F32)],
        [scr((inner, width), BF), pds(2), phs(3), chunk_f, chunk_b, hid_f, hid_b],
        name="encoder_in", us=16,
    )
    parts2, sec_e = lax.optimization_barrier((parts2, sec_e))
    bundle2 = placed_parts(parts2)
    bundle2b = flip(bundle2, "pipe", 1)
    w_conv = [part(bundle2, 2 * PIECE, 0), part(bundle2b, 2 * PIECE, 0)]
    w_outer = [part(bundle2, PIECE, 2), part(bundle2b, PIECE, 2)]
    out_e, xh3_e, dg3_e, inv3_e, third_e, sec_d, xh2_d, dg2_d, inv2_d = call(
        encoder_out, meta, (5,),
        [fixed(sec_e), fixed(codes), fixed(code_cols), rows_chunk(tokens_t)] + halo + w_conv + w_outer + w_inner + last_ins,
        [
            out_chunks(width, F32), out_chunks(inner, BF), out_chunks(inner, BF), out_chunks(8, F32), out_chunks(TILE, BF),
            out_fixed((rows, inner, ext), BF), out_chunks(inner, BF), out_chunks(inner, BF), out_chunks(8, F32),
        ],
        [
            scr((inner, 5 * LANES), BF), scr((width, inner), BF), scr((inner, width), BF), pds(3), phs(6),
            scr((2 * CHUNK, 5 * LANES), BF), hid_f, hid_b, chunk_b, hid_b, chunk_f,
        ],
        name="encoder_out", us=32,
    )
    final = (jax.ShapeDtypeStruct((rows_all, width, length), F32), pl.BlockSpec((2, width, CHUNK), own_index))
    sent = (
        jax.ShapeDtypeStruct((rows, width, length), BF),
        pl.BlockSpec((2, width, CHUNK), lambda c, m: (0, 0, jnp.maximum(c - 1, 0))),
    )
    mine_out, other_out, mixed_d, go_d, gc_d = call(
        decoder_out, meta, (5,),
        [fixed(sec_d), fixed(codes), per_step(out_e), rows_chunk(cotangent_t)] + halo + w_conv + w_outer + last_ins,
        [
            final, sent, out_fixed((rows, inner, ext), BF), out_fixed((width, TILE)), out_fixed((3 * inner, TILE)),
        ],
        [
            scr((inner, 3 * inner), BF), scr((width, inner), BF), scr((inner, width), BF), pds(1), phs(3),
            scr((3 * inner, 2 * CHUNK), BF), hid_f, hid_b, chunk_f, both_b, hid_b, hid_b, hid_b, scr((2, 8, CHUNK), F32), hid_f,
            pds(1), phs(3),
        ],
        name="decoder_out", us=30,
    )
    grad_d, mixed_e, gi_d, go_e = call(
        decoder_back, meta, (5,),
        [
            fixed(mixed_d), fixed(codes), per_step(xh2_d), per_step(dg2_d), per_step(inv2_d), per_step(out_e),
            rows_chunk(cotangent_t),
        ]
        + halo + [per_step(xh3_e), per_step(dg3_e), per_step(inv3_e), per_step(third_e)]
        + w_conv + w_inner + w_outer + last_ins,
        [out_chunks(width, F32), out_fixed((rows, ext, LANES), BF), out_fixed((width, TILE)), out_fixed((width, TILE))],
        [
            scr((inner, 3 * inner), BF), scr((width, inner), BF), scr((inner, width), BF), pds(2), phs(2),
            scr((3 * inner, 2 * CHUNK), BF), hid_f, hid_b, hid_b, both_b, both_b, chunk_f, chunk_f, chunk_f, scr((2, 8, CHUNK), F32), pds(3), phs(6),
        ],
        name="decoder_back", us=40,
    )
    ins5 = (
        [
            fixed(mixed_e), fixed(sec_e), fixed(code_cols), per_step(xh2_e, 4), per_step(dg2_e, 4), per_step(inv2_e, 4),
            (tokens_t, pl.BlockSpec((2, width, CHUNK), lambda c, m: (m[0], 0, c))), per_step(grad_d, 4),
        ]
        + w_conv + w_inner + last_ins
        + [
            (flip(other_out, "pipe", 1), pl.BlockSpec((2, width, CHUNK), lambda c, m: (0, 0, c))),
            fixed(go_e), fixed(gi_d), fixed(go_d), fixed(gc_d),
            (mine_out, pl.BlockSpec(memory_space=pl.ANY)),
        ]
    )
    packed_rows = 2 * width + 4 * inner
    mine_grad, other_grad, kept, sent_grads, section_output = call(
        encoder_back, meta, (4,), ins5,
        [
            (final[0], pl.BlockSpec((2, width, CHUNK), lambda c, m: (m[0], 0, c))),
            (sent[0], pl.BlockSpec((2, width, CHUNK), lambda c, m: (0, 0, c))),
            out_fixed((packed_rows, TILE)), out_fixed((packed_rows, TILE), BF),
            (final[0], pl.BlockSpec((2, width, CHUNK), lambda c, m: (1 - m[0], 0, c))),
        ],
        [
            scr((inner, 5 * LANES), BF), scr((width, inner), BF), pds(2), phs(1),
            scr((2 * CHUNK, 5 * LANES), BF), scr((2 * CHUNK, 5 * LANES), BF), scr((TILE, 5 * LANES), F32), hid_f, hid_b, both_b, chunk_f, chunk_f, chunk_f, scr((2, 8, CHUNK), F32), scr((width, TILE), F32),
            pds(2), phs(3),
        ],
        aliases={len(ins5): 4}, name="encoder_back", us=32,
    )

    def finish(mine, other):
        block = (1, width // 2, length)
        return jnp.transpose(
            call(
                fill_rows, meta, (2 * rows,),
                [
                    (flip(other, "pipe", 1), pl.BlockSpec(block, lambda c, m: (c // 2, c % 2, 0))),
                    (mine, pl.BlockSpec(memory_space=pl.ANY)),
                ],
                [(final[0], pl.BlockSpec(block, lambda c, m: (rows - rows * m[0] + c // 2, c % 2, 0)))],
                aliases={2: 0}, name="fill_rows", us=7,
            )[0],
            (0, 2, 1),
        )

    section_output = jnp.transpose(section_output, (0, 2, 1))[None]

    arrived, other_grad = lax.optimization_barrier((flip(sent_grads, "pipe", 1), other_grad))
    kept = kept + arrived.astype(F32)
    input_gradient = finish(mine_grad, other_grad)[None]
    parts, input_gradient = spread_over(kept, "seq", input_gradient)
    summed = collect_over(parts, "seq")
    grads_inner, grads_outer = summed[:width], summed[width : 2 * width]
    conv_sum = summed[2 * width :]
    conv_other = flip(conv_sum, "pipe", 1)
    summed_f = [x.astype(F32) for x in (grads_inner, grads_outer)]
    conv_first = jnp.where(encoder_side, conv_sum, conv_other)
    conv_second = jnp.where(encoder_side, conv_other, conv_sum)
    grad_conv_e = jnp.concatenate([conv_first, conv_second[:inner]], axis=0)[:, :loc].astype(F32).reshape(5, inner, loc)
    grad_conv_d = conv_second[inner:, :loc].astype(F32).reshape(3, inner, loc)
    grad_inner = summed_f[0][:, :loc]
    grad_outer = jnp.transpose(summed_f[1][:, :loc])
    wide = [summed_f[0][:, FREE], summed_f[0][:, FREE + 1], summed_f[1][:, FREE]]
    narrow = jnp.concatenate([summed_f[0][:inner, FREE + 2 : FREE + 5], summed_f[1][:inner, FREE + 1 : FREE + 4]], axis=1)
    narrow = jnp.transpose(lax.dynamic_slice_in_dim(narrow, tensor * loc, loc, 0))

    return (
        section_output,
        input_gradient,
        wide[0][None],
        wide[1][None],
        grad_inner[None],
        narrow[2][None],
        narrow[0][None],
        narrow[1][None],
        grad_conv_e,
        grad_conv_d,
        narrow[5][None],
        narrow[3][None],
        narrow[4][None],
        grad_outer[None],
        wide[2][None],
    )


def solution(mesh):
    return jax.shard_map(
        on_device,
        mesh=mesh,
        in_specs=(
            P(None, "seq", None),
            P(None, "seq"),
            P(None, "seq"),
            P(None, "seq", None),
            P("pipe", None),
            P("pipe", None),
            P("pipe", None, "tensor"),
            P("pipe", "tensor"),
            P("pipe", "tensor"),
            P("pipe", "tensor"),
            P(None, None, "tensor"),
            P(None, None, "tensor"),
            P("pipe", "tensor"),
            P("pipe", "tensor"),
            P("pipe", "tensor"),
            P("pipe", "tensor", None),
            P("pipe", None),
        ),
        out_specs=(
            P("pipe", None, "seq", None),
            P("pipe", None, "seq", None),
            P("pipe", None),
            P("pipe", None),
            P("pipe", None, "tensor"),
            P("pipe", "tensor"),
            P("pipe", "tensor"),
            P("pipe", "tensor"),
            P(None, None, "tensor"),
            P(None, None, "tensor"),
            P("pipe", "tensor"),
            P("pipe", "tensor"),
            P("pipe", "tensor"),
            P("pipe", "tensor", None),
            P("pipe", None),
        ),
        check_vma=False,
    )
```
